128 devices in a mesh: row: 8 (over z, core), col: 16 (over y, x).
Axes of the slice: x: 4, y: 4, z: 4, core: 2. Of those that a mesh axis runs over, the one named last changes fastest.
Arguments:
- atom_single: bfloat16 [16384, 128], P(('row', 'col')), may hold values from -6 to 6
- atom_token: int32 [16384], P(('row', 'col')), may hold values from 0 to 2047, as said below
- atom_cot: bfloat16 [16384, 128], P(('row', 'col')), may hold values from -6 to 6
- token_cond: bfloat16 [2048, 768], P('row'), may hold values from -6 to 6
- pair: bfloat16 [2048, 2048, 128], P('row', 'col'), may hold values from -12 to 12
- w_pool: bfloat16 [128, 768], replicated, may hold values from -0.5 to 0.5
- w_qkv: bfloat16 [3, 768, 768], P(None, None, 'col'), may hold values from -0.21875 to 0.21875
- w_bias: bfloat16 [128, 16], replicated, may hold values from -0.8 to 0.8
- w_out: bfloat16 [768, 768], P('col'), may hold values from -0.21875 to 0.21875
- w_dec: bfloat16 [768, 128], replicated, may hold values from -0.21875 to 0.21875
Outputs:
- atom_out: bfloat16 [16384, 128], P(('row', 'col'))
- grad_atom: float32 [16384, 128], P(('row', 'col'))
- grad_bias: float32 [128, 16], replicated
The draws below stay inside these ranges and needn't reach their ends.
Inputs may be any that keep to these rules, and one draw needn't show every extreme that they name: `atom_token`: every token has 1 to 24 atoms and some token exactly 24; the atoms stand in no particular order.
All inputs are finite; a program needn't handle non-finite values.
Results may differ from the reference program's by a relative error of at most 0.014.
The reference program's roundings to bfloat16 on the way count: a program that leaves them out, or rounds other values in their place, can miss the bound.
Values may be sent and summed in bfloat16 or wider, within the bound.
No kernel may reach another device: no remote copies, remote signals or barrier semaphores. Data moves between devices by JAX's collectives and lax.ppermute only.
A program may use at most 64 MiB of HBM per device.

```python
import math
import jax
import jax.numpy as jnp
from jax import lax

D = 768
H = 16
CA = 128
CP = 128
HD = 48
NTOK = 2048
NATOM = 16384


def bias_base(key):
    return jnp.clip(0.2 * jax.random.normal(key, (CP, H), jnp.float32), -0.8, 0.8)


def draw_w_bias(key, part):
    return bias_base(key).astype(jnp.bfloat16)


def draw_atom_token(key, part):
    key = jax.random.fold_in(key, 11)
    order = jax.random.permutation(jax.random.fold_in(key, 1), NTOK)
    remaining = NTOK - 4
    moves = jax.random.randint(jax.random.fold_in(key, 2), (remaining // 2,), 0, 8).astype(jnp.int32)
    paired = jnp.stack([8 - moves, 8 + moves], axis=1).reshape(remaining)
    ranked = jnp.concatenate([jnp.array([24, 3, 3, 2], jnp.int32), paired])
    sizes = jnp.zeros((NTOK,), jnp.int32).at[order].set(ranked)
    listed = jnp.repeat(jnp.arange(NTOK, dtype=jnp.int32), sizes, total_repeat_length=NATOM)
    return jax.random.permutation(jax.random.fold_in(key, 3), listed).astype(jnp.int32)


def draw_pair(key, part):
    key = jax.random.fold_in(key, 7)
    values = jnp.clip(jax.random.normal(key, (NTOK, NTOK, CP), jnp.float32), -12.0, 12.0)
    return values.astype(jnp.bfloat16)


def block_levels(rng, extent, shards, smallest, top_value):
    def one(axis_at, blocks):
        steps = jax.random.uniform(jax.random.fold_in(jax.random.fold_in(rng, 6), axis_at), (blocks,), jnp.float32, smallest / len(shards), top_value / len(shards))
        return jnp.repeat(jnp.exp(steps), extent[axis_at] // blocks).reshape((-1,) + (1,) * (len(extent) - axis_at - 1))

    loudness = one(*shards[0])
    for cut in shards[1:]:
        loudness = loudness * one(*cut)
    return loudness


def gaussian(stream_key, shape, spread, most, split=(), kind=jnp.bfloat16):
    drawn = jax.random.normal(stream_key, shape, jnp.float32) * spread
    if len(split) > 0:
        drawn = block_levels(stream_key, shape, split, -0.22, 0.18) * drawn
    return jnp.clip(drawn, min=-most, max=most).astype(kind)


def setup_inputs(seed: int = 0) -> dict:
    splits = jax.random.split(jax.random.key(seed), 11)
    return {
        "atom_single": gaussian(splits[0], (NATOM, CA), 1.0, 6.0, ((0, 128),)),
        "atom_token": draw_atom_token(jax.random.fold_in(splits[10], 71), 0),
        "atom_cot": gaussian(splits[2], (NATOM, CA), 1.0, 6.0, ((0, 128),)),
        "token_cond": gaussian(splits[3], (NTOK, D), 1.0, 6.0, ((0, 8),)),
        "pair": draw_pair(jax.random.fold_in(splits[10], 71), 0),
        "w_pool": gaussian(splits[5], (CA, D), CA ** -0.5, 0.5),
        "w_qkv": gaussian(splits[6], (3, D, D), D ** -0.5, 0.21875, ((2, 16),)),
        "w_bias": draw_w_bias(jax.random.fold_in(splits[10], 71), 0),
        "w_out": gaussian(splits[8], (D, D), D ** -0.5, 0.21875, ((0, 16),)),
        "w_dec": gaussian(splits[9], (D, CA), D ** -0.5, 0.21875),
    }


EPSILON = 1e-05

def layer_norm(single):
    center = single - lax.optimization_barrier(jnp.mean(single, axis=-1, keepdims=True))
    inverse = lax.rsqrt(lax.optimization_barrier(jnp.mean(center * center, axis=-1, keepdims=True)) + EPSILON)
    return (center * inverse, inverse)

def norm_grad(upstream, normal, inverse):
    return inverse * (upstream - lax.optimization_barrier(jnp.mean(upstream, axis=-1, keepdims=True)) - normal * lax.optimization_barrier(jnp.mean(upstream * normal, axis=-1, keepdims=True)))

def split_heads(matrix):
    return jnp.transpose(matrix.reshape(NTOK, H, HD), (1, 0, 2))

def merge_heads(stacked):
    return jnp.transpose(stacked, (1, 0, 2)).reshape(NTOK, D)

def reference(atom_single, atom_token, atom_cot, token_cond, pair, w_pool, w_qkv, w_bias, w_out, w_dec):
    ones_atom = jnp.ones(atom_token.shape, jnp.float32)
    counts = jax.ops.segment_sum(ones_atom, atom_token, num_segments=NTOK)
    sums = jax.ops.segment_sum(atom_single.astype(jnp.float32), atom_token, num_segments=NTOK)
    cot_sums = jax.ops.segment_sum(atom_cot.astype(jnp.float32), atom_token, num_segments=NTOK)
    pooled = (sums / counts[:, None]).astype(jnp.bfloat16)
    cot_pooled = cot_sums.astype(jnp.bfloat16)
    single = token_cond.astype(jnp.float32) + jnp.dot(pooled, w_pool, preferred_element_type=jnp.float32)
    normal, inverse = layer_norm(single)
    normed = normal.astype(jnp.bfloat16)
    queries = jnp.dot(normed, w_qkv[0], preferred_element_type=jnp.float32).astype(jnp.bfloat16)
    keys = jnp.dot(normed, w_qkv[1], preferred_element_type=jnp.float32).astype(jnp.bfloat16)
    values = jnp.dot(normed, w_qkv[2], preferred_element_type=jnp.float32).astype(jnp.bfloat16)
    grad_out = jnp.dot(cot_pooled, w_dec.T, preferred_element_type=jnp.float32)
    grad_update = grad_out.astype(jnp.bfloat16)
    grad_attended = jnp.dot(grad_update, w_out.T, preferred_element_type=jnp.float32).astype(jnp.bfloat16)
    bias = jnp.dot(pair.reshape(NTOK * NTOK, CP), w_bias, preferred_element_type=jnp.float32).astype(jnp.bfloat16)
    bias_heads = jnp.transpose(bias.reshape(NTOK, NTOK, H), (2, 0, 1))
    scale = 1.0 / math.sqrt(HD)

    def per_head(items):
        head_q, head_k, head_v, head_bias, head_grad = items
        logits = jnp.dot(head_q, head_k.T, preferred_element_type=jnp.float32) * scale + head_bias.astype(jnp.float32)
        shifted = jnp.exp(logits - lax.optimization_barrier(jnp.max(logits, axis=-1, keepdims=True)))
        probs = shifted / lax.optimization_barrier(jnp.sum(shifted, axis=-1, keepdims=True))
        probs_low = probs.astype(jnp.bfloat16)
        attended = jnp.dot(probs_low, head_v, preferred_element_type=jnp.float32).astype(jnp.bfloat16)
        grad_probs = jnp.dot(head_grad, head_v.T, preferred_element_type=jnp.float32)
        delta = lax.optimization_barrier(jnp.sum(probs * grad_probs, axis=-1, keepdims=True))
        grad_logits = (probs * (grad_probs - delta)).astype(jnp.bfloat16)
        grad_q = (jnp.dot(grad_logits, head_k, preferred_element_type=jnp.float32) * scale).astype(jnp.bfloat16)
        grad_k = (jnp.dot(grad_logits.T, head_q, preferred_element_type=jnp.float32) * scale).astype(jnp.bfloat16)
        grad_v = jnp.dot(probs_low.T, head_grad, preferred_element_type=jnp.float32).astype(jnp.bfloat16)
        return (attended, grad_logits, grad_q, grad_k, grad_v)
    attended, grad_logits, grad_q, grad_k, grad_v = lax.map(per_head, (split_heads(queries), split_heads(keys), split_heads(values), bias_heads, split_heads(grad_attended)))
    update = jnp.dot(merge_heads(attended), w_out, preferred_element_type=jnp.float32)
    token_out = (single + update).astype(jnp.bfloat16)
    token_back = jnp.dot(token_out, w_dec, preferred_element_type=jnp.float32).astype(jnp.bfloat16)
    atom_out = (atom_single.astype(jnp.float32) + token_back[atom_token].astype(jnp.float32)).astype(jnp.bfloat16)
    logit_rows = jnp.transpose(grad_logits, (1, 2, 0)).reshape(NTOK * NTOK, H)
    grad_bias = jnp.dot(pair.reshape(NTOK * NTOK, CP).T, logit_rows, preferred_element_type=jnp.float32)
    grad_normed = jnp.dot(merge_heads(grad_q), w_qkv[0].T, preferred_element_type=jnp.float32)
    grad_normed = grad_normed + jnp.dot(merge_heads(grad_k), w_qkv[1].T, preferred_element_type=jnp.float32)
    grad_normed = grad_normed + jnp.dot(merge_heads(grad_v), w_qkv[2].T, preferred_element_type=jnp.float32)
    grad_single = (grad_out + norm_grad(grad_normed, normal, inverse)).astype(jnp.bfloat16)
    token_grad = (jnp.dot(grad_single, w_pool.T, preferred_element_type=jnp.float32) / counts[:, None]).astype(jnp.bfloat16)
    grad_atom = atom_cot.astype(jnp.float32) + token_grad[atom_token].astype(jnp.float32)
    return (atom_out, grad_atom, grad_bias)
```

```python
import math

import jax
import jax.numpy as jnp
from jax import lax
from jax.sharding import PartitionSpec as P

HD = 48


EPSILON = 1e-05
BF = jnp.bfloat16
F32 = jnp.float32


def norm_grad(upstream, normal, inverse):
    return inverse * (
        upstream
        - jnp.mean(upstream, axis=-1, keepdims=True)
        - normal * jnp.mean(upstream * normal, axis=-1, keepdims=True)
    )


def nt(left, right):
    return lax.dot_general(left, right, (((1,), (1,)), ((), ())), preferred_element_type=F32)


def tn(left, right):
    return lax.dot_general(left, right, (((0,), (0,)), ((), ())), preferred_element_type=F32)


def nn(left, right):
    return jnp.dot(left, right, preferred_element_type=F32)


def exchange(blocks, axis):
    return lax.all_to_all(blocks, axis, split_axis=0, concat_axis=0, tiled=True)


def spread(block, axis):
    return exchange(jnp.broadcast_to(block[None], (lax.axis_size(axis),) + block.shape), axis)


def split_ids(ids):
    return jnp.concatenate([ids // 64, ids % 64]).astype(BF)[None]


def join_ids(rows):
    half = rows.shape[-1] // 2
    rows = rows.astype(F32)
    return (rows[:, :half] * 64.0 + rows[:, half:]).astype(jnp.int32)


def on_device(
    atom_single, atom_token, atom_cot, token_cond, pair, w_pool, w_qkv, w_bias, w_out, w_dec
):
    rows, cols = lax.axis_size("row"), lax.axis_size("col")
    row, col = lax.axis_index("row"), lax.axis_index("col")
    tok_rows = token_cond.shape[0]
    total_tokens = tok_rows * rows
    n_atoms, width = atom_single.shape
    scale = 1.0 / math.sqrt(HD)
    tile = tok_rows // cols

    own_ids = split_ids(atom_token)
    stacked = jnp.concatenate([atom_single, atom_cot], axis=1)
    payload = jnp.concatenate([stacked, jnp.pad(own_ids, ((0, 15), (0, 0)))], axis=0)
    by_col = spread(payload, "col")

    bias_local = jnp.einsum("ijc,ch->hij", pair, w_bias, preferred_element_type=F32).astype(BF)

    atoms = by_col[:, :n_atoms].reshape(cols * n_atoms, 2 * width)
    ids = join_ids(by_col[:, n_atoms]).reshape(-1)
    onehot = (jnp.arange(total_tokens, dtype=jnp.int32)[:, None] == ids[None, :]).astype(BF)
    partial_sums = nn(onehot, atoms).astype(BF).reshape(rows, tok_rows, 2 * width)
    partial_counts = jnp.sum(onehot.astype(F32), axis=1).astype(BF).reshape(rows, 1, tok_rows)
    extra = jnp.concatenate(
        [
            partial_counts,
            jnp.broadcast_to(own_ids[None], (rows, 1, 2 * width)),
            jnp.zeros((rows, 14, 2 * width), BF),
        ],
        axis=1,
    )
    by_row = exchange(jnp.concatenate([partial_sums, extra], axis=1), "row")
    bias = exchange(bias_local, "col")

    sums = jnp.sum(by_row[:, :tok_rows].astype(F32), axis=0)
    counts = jnp.sum(by_row[:, tok_rows].astype(F32), axis=0)[:, None]
    column_ids = join_ids(by_row[:, tok_rows + 1]).reshape(-1)
    pooled = (sums[:, :width] / counts).astype(BF)
    cot_pooled = sums[:, width:].astype(BF)
    single = token_cond.astype(F32) + nn(pooled, w_pool)
    center = single - jnp.mean(single, axis=-1, keepdims=True)
    inverse = lax.rsqrt(jnp.mean(center * center, axis=-1, keepdims=True) + EPSILON)
    normal = center * inverse
    normed = normal.astype(BF)
    w_t = jnp.transpose(w_qkv, (0, 2, 1))
    queries = nt(normed, w_t[0]).astype(BF)
    kv_t = nt(w_t[1:].reshape(2 * HD, -1), normed).astype(BF)
    kv_all = spread(kv_t, "row")
    keys_t = jnp.transpose(kv_all[:, :HD], (1, 0, 2)).reshape(HD, total_tokens)
    values_t = jnp.transpose(kv_all[:, HD:], (1, 0, 2)).reshape(HD, total_tokens)
    grad_out = nt(cot_pooled, w_dec)
    grad_attended = nt(grad_out.astype(BF), w_out).astype(BF)

    bias_rows = jnp.transpose(bias, (1, 0, 2)).reshape(tok_rows, total_tokens)
    logits = nn(queries, keys_t) * scale + bias_rows.astype(F32)
    shifted = jnp.exp(logits - jnp.max(logits, axis=-1, keepdims=True))
    probs = shifted / jnp.sum(shifted, axis=-1, keepdims=True)
    probs_low = probs.astype(BF)
    attended = nt(probs_low, values_t).astype(BF)
    grad_probs = nn(grad_attended, values_t)
    delta = jnp.sum(probs * grad_probs, axis=-1, keepdims=True)
    grad_logits = (probs * (grad_probs - delta)).astype(BF)
    grad_queries = (nt(grad_logits, keys_t) * scale).astype(BF)
    gk_t = tn(queries, grad_logits)
    gv_t = tn(grad_attended, probs_low)
    gkv_t = jnp.transpose(
        jnp.concatenate([gk_t, gv_t], axis=0).astype(BF).reshape(2 * HD, rows, tok_rows), (1, 0, 2)
    )
    gkv_parts = exchange(gkv_t, "row")
    logits_back = jnp.transpose(
        grad_logits.reshape(tok_rows, cols, total_tokens // cols), (1, 0, 2)
    )
    bias_back = exchange(logits_back, "col")

    update = nn(attended, w_out).astype(BF)
    back_parts = exchange(nn(update, w_dec).astype(BF).reshape(cols, tile, width), "col")
    single_tile = lax.dynamic_slice_in_dim(single, col * tile, tile, 0)
    back_tile = (
        nn(single_tile.astype(BF), w_dec) + jnp.sum(back_parts.astype(F32), axis=0)
    ).astype(BF)

    gkv = jnp.sum(gkv_parts.astype(F32), axis=0)
    grad_keys = (gkv[:HD] * scale).astype(BF)
    grad_values = gkv[HD:].astype(BF)
    normed_part = nn(grad_queries, w_t[0]) + tn(grad_keys, w_t[1]) + tn(grad_values, w_t[2])
    base = jnp.where(col == 0, grad_out, 0.0)
    single_part = (base + norm_grad(normed_part, normal, inverse)).astype(BF)
    grad_part = (nt(single_part, w_pool) / counts).astype(BF)

    weight_part = jnp.einsum("ijc,hij->hc", pair, bias_back, preferred_element_type=F32)
    high = weight_part.astype(BF)
    low = (weight_part - high.astype(F32)).astype(BF)
    parts = spread(jnp.concatenate([grad_part, back_tile, high, low], axis=0), "col")
    token_grad = jnp.sum(parts[:, :tok_rows].astype(F32), axis=0).astype(BF)
    token_back = parts[:, tok_rows : tok_rows + tile].reshape(tok_rows, width)
    weight_row = jnp.sum(parts[:, tok_rows + tile :].astype(F32), axis=0)
    weight_row = weight_row[:16] + weight_row[16:]

    local_ids = column_ids - row * tok_rows
    pick = (local_ids[:, None] == jnp.arange(tok_rows, dtype=jnp.int32)[None, :]).astype(BF)
    picked = nn(pick, jnp.concatenate([token_back, token_grad], axis=1)).astype(BF)
    high = weight_row.astype(BF)
    low = (weight_row - high.astype(F32)).astype(BF)
    tail = jnp.broadcast_to(jnp.concatenate([high, low], axis=1)[None], (rows, 16, 2 * width))
    final = exchange(
        jnp.concatenate([picked.reshape(rows, n_atoms, 2 * width), tail], axis=1), "row"
    )
    final = jnp.sum(final.astype(F32), axis=0)
    atom_out = (atom_single.astype(F32) + final[:n_atoms, :width]).astype(BF)
    grad_atom = atom_cot.astype(F32) + final[:n_atoms, width:]
    grad_bias = jnp.transpose(final[n_atoms:, :width] + final[n_atoms:, width:])
    return (atom_out, grad_atom, grad_bias)


def solution(mesh):
    return jax.shard_map(
        on_device,
        mesh=mesh,
        in_specs=(
            P(("row", "col"), None),
            P(("row", "col")),
            P(("row", "col"), None),
            P("row", None),
            P("row", "col", None),
            P(),
            P(None, None, "col"),
            P(),
            P("col", None),
            P(),
        ),
        out_specs=(P(("row", "col"), None), P(("row", "col"), None), P()),
        check_vma=False,
    )
```

```python
import math

import jax
import jax.numpy as jnp
from jax import lax
from jax.experimental import pallas as pl
from jax.experimental.pallas import tpu as pltpu
from jax.sharding import PartitionSpec as P

HD = 48


EPSILON = 1e-05
BF = jnp.bfloat16
F32 = jnp.float32


def nt(left, right):
    return lax.dot_general(left, right, (((1,), (1,)), ((), ())), preferred_element_type=F32)


def tn(left, right):
    return lax.dot_general(left, right, (((0,), (0,)), ((), ())), preferred_element_type=F32)


def nn(left, right):
    return jnp.dot(left, right, preferred_element_type=F32)


def exchange(blocks, axis):
    return lax.all_to_all(blocks, axis, split_axis=0, concat_axis=0, tiled=True)


def spread(block, axis):
    return exchange(jnp.broadcast_to(block[None], (lax.axis_size(axis),) + block.shape), axis)


def after(value, *others):
    return lax.optimization_barrier((value,) + others)[0]


def high_low(value):
    high = value.astype(BF)
    return [high, (value - high.astype(F32)).astype(BF)]


def norm_kernel(at, cond_ref, pooled_ref, wpool_ref, wt_ref, normed_ref, inv_ref, kv_ref, q_ref, qt_ref):
    single = cond_ref[...].astype(F32) + nn(pooled_ref[...], wpool_ref[...])
    center = single - jnp.mean(single, axis=-1, keepdims=True)
    inverse = lax.rsqrt(jnp.mean(center * center, axis=-1, keepdims=True) + EPSILON)
    normed = (center * inverse).astype(BF)
    normed_ref[...] = normed
    inv_ref[...] = inverse
    kv_ref[...] = nt(wt_ref[HD:], normed).astype(BF)

    @pl.when(pl.program_id(0) == at[0])
    def _():
        q_ref[...] = nt(normed, wt_ref[:HD]).astype(BF)
        qt_ref[...] = nt(wt_ref[:HD], normed).astype(BF)


def norm_tokens(at, cond, pooled, w_pool, w_t, rows):
    tokens, features = cond.shape
    block = tokens // rows
    whole = lambda shape: pl.BlockSpec(shape, lambda b: (0, 0))
    return pl.pallas_call(
        norm_kernel,
        grid=(rows,),
        in_specs=[
            pl.BlockSpec(memory_space=pltpu.SMEM),
            pl.BlockSpec((block, features), lambda b: (b, 0)),
            pl.BlockSpec((block, pooled.shape[1]), lambda b: (b, 0)),
            whole(w_pool.shape),
            whole(w_t.shape),
        ],
        out_specs=[
            pl.BlockSpec((block, features), lambda b: (b, 0)),
            pl.BlockSpec((block, 1), lambda b: (b, 0)),
            pl.BlockSpec((2 * HD, block), lambda b: (0, b)),
            whole((block, HD)),
            whole((HD, block)),
        ],
        out_shape=[
            jax.ShapeDtypeStruct((tokens, features), BF),
            jax.ShapeDtypeStruct((tokens, 1), F32),
            jax.ShapeDtypeStruct((2 * HD, tokens), BF),
            jax.ShapeDtypeStruct((block, HD), BF),
            jax.ShapeDtypeStruct((HD, block), BF),
        ],
        compiler_params=pltpu.CompilerParams(vmem_limit_bytes=24 * 2**20),
        cost_estimate=pl.CostEstimate(
            flops=2 * tokens * features * 272, bytes_accessed=8 * 2**20, transcendentals=0
        ),
    )(at, cond, pooled, w_pool, w_t)


def attend_kernel(
    at, q_ref, qt_ref, kv_ref, bias_ref, wt_ref, normed_ref, inv_ref, wpool_ref, wout_ref, wdec_ref,
    out_ref, s_ref, g_ref, u_ref,
):
    scale = 1.0 / math.sqrt(HD)
    blocks, tokens, columns = s_ref.shape
    half = columns // 2
    cols = 2 * blocks
    tile = tokens // cols
    spans = [slice(b * columns, (b + 1) * columns) for b in range(blocks)]

    queries = q_ref[...]
    top = jnp.full((tokens, 1), -jnp.inf, F32)
    for b in range(blocks):
        bias = jnp.concatenate([bias_ref[2 * b, :tokens], bias_ref[2 * b + 1, :tokens]], axis=1)
        logits = nn(queries, kv_ref[:HD, spans[b]]) * scale + bias.astype(F32)
        s_ref[b] = logits
        top = jnp.maximum(top, jnp.max(logits, axis=-1, keepdims=True))
    total = jnp.zeros((tokens, 1), F32)
    for b in range(blocks):
        shifted = jnp.exp(s_ref[b] - top)
        s_ref[b] = shifted
        total = total + jnp.sum(shifted, axis=-1, keepdims=True)
    share = 1.0 / total

    cots = jnp.concatenate([bias_ref[c, tokens : tokens + tile] for c in range(cols)], axis=0)
    grad_out = nt(cots, wdec_ref[...])
    grad_low = grad_out.astype(BF)
    grad_att = nt(grad_low, wout_ref[...]).astype(BF)
    grad_att_t = nt(wout_ref[...], grad_low).astype(BF)
    attended = jnp.zeros((tokens, HD), F32)
    delta = jnp.zeros((tokens, 1), F32)
    for b in range(blocks):
        probs = s_ref[b] * share
        s_ref[b] = probs
        values = kv_ref[HD:, spans[b]]
        attended = attended + nt(probs.astype(BF), values)
        grad_probs = nn(grad_att, values)
        g_ref[b] = grad_probs
        delta = delta + jnp.sum(probs * grad_probs, axis=-1, keepdims=True)
    update = nn(attended.astype(BF), wout_ref[...]).astype(BF)
    back = nn(update, wdec_ref[...]).astype(BF)
    for c in range(cols):
        out_ref[c, tokens + half : tokens + half + tile] = back[c * tile : (c + 1) * tile]

    grad_queries = jnp.zeros((tokens, HD), F32)
    for b in range(blocks):
        probs = s_ref[b]
        low = (probs * (g_ref[b] - delta)).astype(BF)
        out_ref[2 * b, :tokens] = low[:, :half]
        out_ref[2 * b + 1, :tokens] = low[:, half:]
        grad_queries = grad_queries + nt(low, kv_ref[:HD, spans[b]])
        grad_k = (nn(qt_ref[...], low) * scale).astype(BF)
        grad_v = nn(grad_att_t, probs.astype(BF)).astype(BF)
        u_ref[b] = tn(jnp.concatenate([grad_k, grad_v], axis=0), wt_ref[HD:])
    own = nn((grad_queries * scale).astype(BF), wt_ref[:HD])
    u_ref[at[0]] += own
    first = (at[1] == 0).astype(F32)
    for b in range(blocks):
        upstream = u_ref[b]
        normal = normed_ref[spans[b]].astype(F32)
        part = inv_ref[spans[b]] * (
            upstream
            - jnp.mean(upstream, axis=-1, keepdims=True)
            - normal * jnp.mean(upstream * normal, axis=-1, keepdims=True)
        )
        here = first * (at[0] == b).astype(F32)
        part = nt((part + grad_out * here).astype(BF), wpool_ref[...]).astype(BF)
        out_ref[2 * b, tokens : tokens + half] = part[:half]
        out_ref[2 * b + 1, tokens : tokens + half] = part[half:]


def attend(at, queries, queries_t, kv_t, bias, w_t, normed, inverse, w_pool, w_out, w_dec, rows):
    tokens = queries.shape[0]
    features = w_t.shape[1]
    cols, _, half = bias.shape
    vmem = pl.BlockSpec(memory_space=pltpu.VMEM)
    return pl.pallas_call(
        attend_kernel,
        in_specs=[pl.BlockSpec(memory_space=pltpu.SMEM)] + [vmem] * 10,
        out_specs=vmem,
        out_shape=jax.ShapeDtypeStruct((cols, tokens + half + tokens // cols, half), BF),
        scratch_shapes=[
            pltpu.VMEM((rows, tokens, 2 * half), F32),
            pltpu.VMEM((rows, tokens, 2 * half), F32),
            pltpu.VMEM((rows, tokens, features), F32),
        ],
        compiler_params=pltpu.CompilerParams(vmem_limit_bytes=40 * 2**20),
        cost_estimate=pl.CostEstimate(
            flops=2 * 10**9, bytes_accessed=8 * 2**20, transcendentals=2**19
        ),
    )(at, queries, queries_t, kv_t, bias, w_t, normed, inverse, w_pool, w_out, w_dec)


def on_device(
    atom_single, atom_token, atom_cot, token_cond, pair, w_pool, w_qkv, w_bias, w_out, w_dec
):
    rows, cols = lax.axis_size("row"), lax.axis_size("col")
    row, col = lax.axis_index("row"), lax.axis_index("col")
    tok_rows = token_cond.shape[0]
    total_tokens = tok_rows * rows
    n_atoms, width = atom_single.shape
    tile = tok_rows // cols

    everyone = ("row", "col")
    devices = rows * cols
    cond_all = lax.all_gather(token_cond, "row", axis=0, tiled=True)
    onehot = (
        jnp.arange(total_tokens, dtype=jnp.int32)[:, None] == atom_token[None, :]
    ).astype(BF)
    with_ones = jnp.concatenate([atom_single, atom_cot, jnp.ones_like(atom_single)], axis=1)
    partial = nn(onehot, with_ones).reshape(devices, tile, 3 * width)
    place = jnp.eye(tile, width, dtype=F32)
    partial_counts = jnp.sum(partial[:, :, 2 * width :] * place, axis=1, keepdims=True)
    to_tiles = jnp.concatenate(
        [
            partial[:, :, :width].astype(BF),
            partial[:, :, width : 2 * width].astype(BF),
            jnp.pad(partial_counts.astype(BF), ((0, 0), (0, 7), (0, 0))),
        ],
        axis=1,
    )
    from_all = exchange(to_tiles, everyone)
    bias_local = jnp.einsum("ijc,ch->hij", pair, w_bias, preferred_element_type=F32).astype(BF)
    from_all = after(from_all, bias_local)
    sums = jnp.sum(from_all.astype(F32), axis=0)
    tile_counts = jnp.sum(sums[2 * tile : 2 * tile + 1] * place, axis=1, keepdims=True)
    pooled_tile = (sums[:tile] / tile_counts).astype(BF)
    cot_tile = sums[tile : 2 * tile].astype(BF)
    pooled = spread(pooled_tile, everyone).reshape(total_tokens, width)
    lanes = jnp.arange(width, dtype=jnp.int32)[None]
    seat = jnp.arange(tile, dtype=jnp.int32)[:, None] + tile * (col % (cols // 2))
    count_row = jnp.sum(jnp.where(lanes == seat, tile_counts, 0.0), axis=0, keepdims=True)
    count_row = jnp.where(jnp.arange(tile)[:, None] == col // (cols // 2), count_row, 0.0)
    shared = jnp.broadcast_to(
        jnp.concatenate([cot_tile, count_row.astype(BF)], axis=0)[None], (cols, 2 * tile, width)
    )
    bias_cot = exchange(after(jnp.concatenate([bias_local, shared], axis=1), pooled), "col")

    at = jnp.stack([row, col]).astype(jnp.int32)
    w_t = jnp.transpose(w_qkv, (0, 2, 1)).reshape(3 * HD, -1)
    normed, inverse, kv_t, queries, queries_t = norm_tokens(
        at, cond_all, pooled, w_pool, w_t, rows
    )
    at_tile = row * tok_rows + col * tile
    single_tile = lax.dynamic_slice_in_dim(cond_all, at_tile, tile, 0).astype(F32) + nn(
        pooled_tile, w_pool
    )
    tile_base = nn(single_tile.astype(BF), w_dec)
    bias_cot = after(bias_cot, kv_t, tile_base)
    row_counts = jnp.sum(bias_cot[:, tok_rows + tile : tok_rows + tile + 2].astype(F32), axis=0)
    columns = total_tokens // cols
    block_counts = jnp.where(
        row == col // 2, lax.dynamic_slice_in_dim(row_counts, col % 2, 1, 0), 0.0
    ).astype(BF)

    hop = attend(
        at, queries, queries_t, kv_t, bias_cot, w_t, normed, inverse, w_pool, w_out, w_dec, rows
    )
    hop = exchange(hop, "col")
    bias_back = hop[:, :tok_rows]
    rest = jnp.sum(hop[:, tok_rows:].astype(F32), axis=0)
    weight_part = jnp.einsum("ijc,hij->hc", pair, bias_back, preferred_element_type=F32)
    heads = weight_part.shape[0]
    hop = spread(
        jnp.concatenate(
            [rest[:columns].astype(BF), (tile_base + rest[columns:]).astype(BF)]
            + high_low(weight_part)
            + [jnp.pad(block_counts, ((0, 15), (0, 0)))],
            axis=0,
        ),
        "row",
    )
    at_counts = columns + tile + 2 * heads
    count_row = jnp.sum(hop[:, at_counts : at_counts + 1].astype(F32), axis=0)
    own_counts = jnp.sum(count_row * jnp.eye(columns, dtype=F32), axis=1, keepdims=True)
    token_grad = (jnp.sum(hop[:, :columns].astype(F32), axis=0) / own_counts).astype(BF)
    token_back = hop[:, columns : columns + tile].reshape(columns, width)
    weight_col = jnp.sum(hop[:, columns + tile : at_counts].astype(F32), axis=0)
    hop = spread(
        jnp.concatenate(
            [token_grad, token_back] + high_low(weight_col[:heads] + weight_col[heads:]), axis=0
        ),
        "col",
    )
    grad_table = hop[:, :columns].reshape(total_tokens, width)
    back_table = hop[:, columns : 2 * columns].reshape(total_tokens, width)
    weight = jnp.sum(hop[:, 2 * columns :].astype(F32), axis=0)
    of_row, rest = atom_token // tok_rows, atom_token % tok_rows
    back_ids = (rest // tile) * columns + of_row * tile + rest % tile
    slots = jnp.arange(total_tokens, dtype=jnp.int32)[None, :]
    grad_atom = atom_cot.astype(F32) + nn((atom_token[:, None] == slots).astype(BF), grad_table)
    atom_out = (
        atom_single.astype(F32) + nn((back_ids[:, None] == slots).astype(BF), back_table)
    ).astype(BF)
    grad_bias = jnp.transpose(weight[:heads] + weight[heads:])
    return (atom_out, grad_atom, grad_bias)


def solution(mesh):
    return jax.shard_map(
        on_device,
        mesh=mesh,
        in_specs=(
            P(("row", "col"), None),
            P(("row", "col")),
            P(("row", "col"), None),
            P("row", None),
            P("row", "col", None),
            P(),
            P(None, None, "col"),
            P(),
            P("col", None),
            P(),
        ),
        out_specs=(P(("row", "col"), None), P(("row", "col"), None), P()),
        check_vma=False,
    )
```

```python
import math

import jax
import jax.numpy as jnp
from jax import lax
from jax.experimental import pallas as pl
from jax.experimental.pallas import tpu as pltpu
from jax.sharding import Mesh
from jax.sharding import PartitionSpec as P

HD = 48


EPSILON = 1e-05
BF = jnp.bfloat16
F32 = jnp.float32


def nt(left, right):
    return lax.dot_general(left, right, (((1,), (1,)), ((), ())), preferred_element_type=F32)


def tn(left, right):
    return lax.dot_general(left, right, (((0,), (0,)), ((), ())), preferred_element_type=F32)


def nn(left, right):
    return jnp.dot(left, right, preferred_element_type=F32)


def exchange(blocks, axis):
    return lax.all_to_all(blocks, axis, split_axis=0, concat_axis=0, tiled=True)


def spread(block, axis):
    return exchange(jnp.broadcast_to(block[None], (lax.axis_size(axis),) + block.shape), axis)


def after(value, *others):
    return lax.optimization_barrier((value,) + others)[0]


def high_low(value):
    high = value.astype(BF)
    return [high, (value - high.astype(F32)).astype(BF)]


def norm_kernel(
    at, cond0, cond1, cond2, cond3, cond4, cond5, cond6, cond7, pooled_ref, pooled_other, wt_ref,
    wpool_ref, normed_ref, inv_ref, kv_ref, q_ref, qt_ref,
):
    cols, half, _ = normed_ref.shape
    conds = (cond0, cond1, cond2, cond3, cond4, cond5, cond6, cond7)
    for step in range(cols // 2):
        at_z = jnp.bitwise_xor(at[2], step // 2)
        b = 2 * at_z + jnp.bitwise_xor(at[3], step % 2)
        pools = pooled_other if step % 2 else pooled_ref
        single = conds[step][...].astype(F32) + nn(pools[at_z], wpool_ref[...])
        center = single - jnp.mean(single, axis=-1, keepdims=True)
        inverse = lax.rsqrt(jnp.mean(center * center, axis=-1, keepdims=True) + EPSILON)
        normed = (center * inverse).astype(BF)
        kv = nt(wt_ref[HD:], normed).astype(BF)
        for i in range(2):
            part = slice(i * half, (i + 1) * half)
            normed_ref[2 * b + i] = normed[part]
            inv_ref[2 * b + i] = inverse[part]
            kv_ref[2 * b + i] = kv[:, part]
        if step == 0:
            q_ref[...] = nt(normed, wt_ref[:HD]).astype(BF)
            qt_ref[...] = nt(wt_ref[:HD], normed).astype(BF)


def attend_kernel(
    q_ref, qt_ref, kv_ref, bias_ref, wout_ref, wdec_ref,
    out_ref, gkv_ref, gq_ref, att_ref, gout_ref, s_ref, g_ref,
):
    scale = 1.0 / math.sqrt(HD)
    blocks, tokens, columns = s_ref.shape
    half = columns // 2
    cols = 2 * blocks
    tile = tokens // cols

    def pair(ref, b, rows):
        return jnp.concatenate([ref[2 * b, rows], ref[2 * b + 1, rows]], axis=1)

    keys, values = slice(0, HD), slice(HD, 2 * HD)
    queries = q_ref[...]
    top = jnp.full((tokens, 1), -jnp.inf, F32)
    for b in range(blocks):
        bias = pair(bias_ref, b, slice(0, tokens))
        logits = nn(queries, pair(kv_ref, b, keys)) * scale + bias.astype(F32)
        s_ref[b] = logits
        top = jnp.maximum(top, jnp.max(logits, axis=-1, keepdims=True))
    total = jnp.zeros((tokens, 1), F32)
    for b in range(blocks):
        shifted = jnp.exp(s_ref[b] - top)
        s_ref[b] = shifted
        total = total + jnp.sum(shifted, axis=-1, keepdims=True)
    share = 1.0 / total

    cots = jnp.concatenate([bias_ref[c, tokens : tokens + tile] for c in range(cols)], axis=0)
    grad_out = nt(cots, wdec_ref[...])
    gout_ref[...] = grad_out
    grad_low = grad_out.astype(BF)
    grad_att = nt(grad_low, wout_ref[...]).astype(BF)
    grad_att_t = nt(wout_ref[...], grad_low).astype(BF)
    attended = jnp.zeros((tokens, HD), F32)
    delta = jnp.zeros((tokens, 1), F32)
    for b in range(blocks):
        probs = s_ref[b] * share
        s_ref[b] = probs
        block = pair(kv_ref, b, values)
        attended = attended + nt(probs.astype(BF), block)
        grad_probs = nn(grad_att, block)
        g_ref[b] = grad_probs
        delta = delta + jnp.sum(probs * grad_probs, axis=-1, keepdims=True)
    att_ref[...] = attended.astype(BF)

    grad_queries = jnp.zeros((tokens, HD), F32)
    for b in range(blocks):
        probs = s_ref[b]
        low = (probs * (g_ref[b] - delta)).astype(BF)
        out_ref[2 * b] = low[:, :half]
        out_ref[2 * b + 1] = low[:, half:]
        grad_queries = grad_queries + nt(low, pair(kv_ref, b, keys))
        grad_k = (nn(qt_ref[...], low) * scale).astype(BF)
        grad_v = nn(grad_att_t, probs.astype(BF)).astype(BF)
        gkv_ref[:, b * columns : (b + 1) * columns] = jnp.concatenate([grad_k, grad_v], axis=0)
    gq_ref[...] = (grad_queries * scale).astype(BF)


def token_grad_kernel(
    at, gkv_ref, gq_ref, att_ref, gout_ref, normed_ref, inv_ref, wt_ref, wpool_ref, wout_ref,
    wdec_ref, mine_ref, other_ref, back_ref, u_ref,
):
    cols, half, _ = normed_ref.shape
    tile, short = back_ref.shape[1], half // 2
    row, col, core = at[0], at[1], at[3]
    update = nn(att_ref[...], wout_ref[...]).astype(BF)
    back = nn(update, wdec_ref[...]).astype(BF)
    for c in range(cols):
        back_ref[c] = back[c * tile : (c + 1) * tile]
    for b in range(cols // 2):
        columns = slice(2 * b * half, 2 * (b + 1) * half)
        upstream = tn(gkv_ref[:, columns], wt_ref[HD:])
        u_ref[2 * b] = upstream[:half]
        u_ref[2 * b + 1] = upstream[half:]
    own = nn(gq_ref[...], wt_ref[:HD])
    u_ref[2 * row] += own[:half]
    u_ref[2 * row + 1] += own[half:]
    head = (col == 0).astype(F32)
    for c in range(cols):
        upstream = u_ref[c]
        normal = normed_ref[c].astype(F32)
        part = inv_ref[c] * (
            upstream
            - jnp.mean(upstream, axis=-1, keepdims=True)
            - normal * jnp.mean(upstream * normal, axis=-1, keepdims=True)
        )
        here = head * (row == c // 2).astype(F32)
        at_half = (c % 2) * half
        part = part + gout_ref[at_half : at_half + half] * here
        grad = nt(part.astype(BF), wpool_ref[...])
        mine_ref[c] = jnp.where(core == 0, grad[:short], grad[short:])
        other_ref[c] = jnp.where(core == 0, grad[short:], grad[:short]).astype(BF)


def call(body, outs, scratch, cost, *args, scalars=None):
    n_in, n_out, n_at = len(args), len(outs), int(scalars is not None)

    def kernel(*refs):
        at, refs = refs[:n_at], refs[n_at:]
        sources, results = refs[:n_in], refs[n_in : n_in + n_out]
        held = refs[n_in + n_out : 2 * (n_in + n_out)]
        sems, rest = refs[2 * (n_in + n_out)], refs[2 * (n_in + n_out) + 1 :]
        incoming = [
            pltpu.make_async_copy(src, dst, sems.at[i])
            for i, (src, dst) in enumerate(zip(sources, held[:n_in]))
        ]
        for copy in incoming:
            copy.start()
        for copy in incoming:
            copy.wait()
        body(*at, *held, *rest)
        outgoing = [
            pltpu.make_async_copy(src, dst, sems.at[n_in + i])
            for i, (src, dst) in enumerate(zip(held[n_in:], results))
        ]
        for copy in outgoing:
            copy.start()
        for copy in outgoing:
            copy.wait()

    anywhere = pl.BlockSpec(memory_space=pl.ANY)
    specs = [pl.BlockSpec(memory_space=pltpu.SMEM)] * n_at + [anywhere] * n_in
    return pl.pallas_call(
        kernel,
        in_specs=specs,
        out_specs=[anywhere] * n_out,
        out_shape=[jax.ShapeDtypeStruct(*out) for out in outs],
        scratch_shapes=[pltpu.VMEM(arg.shape, arg.dtype) for arg in args]
        + [pltpu.VMEM(*out) for out in outs]
        + [pltpu.SemaphoreType.DMA((n_in + n_out,))]
        + [pltpu.VMEM(*item) for item in scratch],
        compiler_params=pltpu.CompilerParams(vmem_limit_bytes=56 * 2**20),
        cost_estimate=pl.CostEstimate(
            flops=cost, bytes_accessed=8 * 2**20, transcendentals=2**19
        ),
    )(*([scalars] * n_at), *args)


ROW, COL, SAME_CORE = ("z", "k"), ("y", "x"), ("z", "y", "x")
SWAP = [(0, 1), (1, 0)]


def turn(value, axis, by):
    size = lax.axis_size(axis)
    return lax.ppermute(value, axis, [(i, i ^ by) for i in range(size)])


def take(value, start, size, axis=0):
    return lax.dynamic_slice_in_dim(value, start, size, axis)


def on_device(
    atom_single, atom_token, atom_cot, token_cond, pair, w_pool, w_qkv, w_bias, w_out, w_dec
):
    side = lax.axis_size("x")
    rows, cols = lax.axis_size("z") * 2, lax.axis_size("y") * side
    z, core, y, x = [lax.axis_index(name) for name in ("z", "k", "y", "x")]
    row, col = z * 2 + core, y * side + x
    tok_rows = token_cond.shape[0]
    total_tokens = tok_rows * rows
    n_atoms, width = atom_single.shape
    tile, columns = tok_rows // cols, total_tokens // cols
    peers = rows * cols // 2
    at = jnp.stack([row, col, z, core]).astype(jnp.int32)
    w_t = jnp.transpose(w_qkv, (0, 2, 1)).reshape(3 * HD, -1)

    own_atoms = jnp.concatenate([atom_single, atom_cot], axis=1)
    atoms = jnp.concatenate([own_atoms, lax.ppermute(own_atoms, "k", SWAP)], axis=0)
    ids = jnp.concatenate([atom_token, lax.ppermute(atom_token, "k", SWAP)])
    slots = jnp.arange(total_tokens // 2, dtype=jnp.int32)
    slots = (slots // tok_rows * 2 + core) * tok_rows + slots % tok_rows
    onehot = (slots[:, None] == ids[None, :]).astype(BF)
    with_ones = jnp.concatenate([atoms, jnp.ones((2 * n_atoms, width), BF)], axis=1)
    partial = nn(onehot, with_ones).reshape(peers, tile, 3 * width)
    place = jnp.eye(tile, width, dtype=F32)
    partial_counts = jnp.sum(partial[:, :, 2 * width :] * place, axis=1, keepdims=True)
    to_tiles = jnp.concatenate(
        [
            partial[:, :, :width].astype(BF),
            partial[:, :, width : 2 * width].astype(BF),
            jnp.pad(partial_counts.astype(BF), ((0, 0), (0, 7), (0, 0))),
        ],
        axis=1,
    )

    bias = jnp.einsum("ijc,ch->hij", pair, w_bias, preferred_element_type=F32).astype(BF)
    from_all = exchange(to_tiles, SAME_CORE)
    late_cond = after(token_cond, to_tiles)
    cond = [token_cond] + [turn(late_cond, "z", d) for d in (1, 2, 3)]
    from_all = after(from_all, bias)
    sums = jnp.sum(from_all.astype(F32), axis=0)
    tile_counts = jnp.sum(sums[2 * tile : 2 * tile + 1] * place, axis=1, keepdims=True)
    pooled_tile = (sums[:tile] / tile_counts).astype(BF)
    lanes = jnp.arange(width, dtype=jnp.int32)[None]
    seat = jnp.arange(tile, dtype=jnp.int32)[:, None] + tile * (col % (cols // 2))
    count_row = jnp.sum(jnp.where(lanes == seat, tile_counts, 0.0), axis=0, keepdims=True)
    count_row = jnp.where(jnp.arange(8)[:, None] == col // (cols // 2), count_row, 0.0)
    count_row = jnp.pad(count_row[:2], ((0, tile - 2), (0, 0)))
    shared = jnp.concatenate([sums[tile : 2 * tile], count_row], axis=0).astype(BF)
    shared = jnp.broadcast_to(shared[None], (cols, 2 * tile, width))
    pooled = spread(pooled_tile, SAME_CORE)
    conds = []
    for piece in cond:
        conds += [piece, lax.ppermute(piece, "k", SWAP)]
    pooled = after(pooled, *conds).reshape(rows // 2, tok_rows, width)
    bias_cot = exchange(after(jnp.concatenate([bias, shared], axis=1), pooled), COL)
    other_pooled = lax.ppermute(pooled, "k", SWAP)
    single_tile = take(token_cond, col * tile, tile).astype(F32) + nn(pooled_tile, w_pool)
    tile_base = nn(single_tile.astype(BF), w_dec)
    features = w_t.shape[1]
    normed, inverse, kv, queries, queries_t = call(
        norm_kernel,
        [
            ((cols, columns, features), BF),
            ((cols, columns, 1), F32),
            ((cols, 2 * HD, columns), BF),
            ((tok_rows, HD), BF),
            ((HD, tok_rows), BF),
        ],
        [], 10**9, *conds, pooled, other_pooled, w_t, w_pool, scalars=at,
    )
    bias_cot = after(bias_cot, kv, tile_base)
    row_counts = jnp.sum(bias_cot[:, tok_rows + tile : tok_rows + tile + 2].astype(F32), axis=0)
    block_counts = jnp.where(row == col // 2, take(row_counts, col % 2, 1), 0.0).astype(BF)

    spread_logits = (rows, tok_rows, 2 * columns)
    grad_logits, grad_kv, grad_queries, attended, grad_out = call(
        attend_kernel,
        [
            ((cols, tok_rows, columns), BF),
            ((2 * HD, total_tokens), BF),
            ((tok_rows, HD), BF),
            ((tok_rows, HD), BF),
            ((tok_rows, features), F32),
        ],
        [(spread_logits, F32), (spread_logits, F32)],
        2 * 10**9, queries, queries_t, kv, bias_cot, w_out, w_dec,
    )
    bias_back = exchange(grad_logits, COL)
    mine, other, back = call(
        token_grad_kernel,
        [
            ((cols, columns // 2, width), F32),
            ((cols, columns // 2, width), BF),
            ((cols, tile, width), BF),
        ],
        [((cols, columns, features), F32)],
        10**9,
        grad_kv, grad_queries, attended, grad_out, normed, inverse, w_t, w_pool, w_out, w_dec,
        scalars=at,
    )
    grad_part = (mine + lax.ppermute(other, "k", SWAP).astype(F32)).astype(BF)
    to_col = jnp.concatenate([grad_part, back], axis=1)
    bias_back = after(bias_back, to_col)
    hop = exchange(after(to_col, bias_back), COL)
    weight_part = jnp.einsum("ijc,hij->hc", pair, bias_back, preferred_element_type=F32)
    hop = after(hop, weight_part)
    rest = jnp.sum(hop.astype(F32), axis=0)
    heads = weight_part.shape[0]
    hop = spread(
        jnp.concatenate(
            [rest[: columns // 2].astype(BF), (tile_base + rest[columns // 2 :]).astype(BF)]
            + high_low(weight_part)
            + [jnp.pad(block_counts, ((0, 15), (0, 0)))],
            axis=0,
        ),
        ROW,
    )
    at_back = columns // 2
    at_weight = at_back + tile
    at_counts = at_weight + 2 * heads
    count_row = jnp.sum(hop[:, at_counts : at_counts + 1].astype(F32), axis=0)
    own_counts = jnp.sum(count_row * jnp.eye(columns, dtype=F32), axis=1, keepdims=True)
    halves = hop[:, :at_back].reshape(rows // 2, columns, width)
    token_grad = (jnp.sum(halves.astype(F32), axis=0) / own_counts).astype(BF)
    token_back = hop[:, at_back:at_weight].reshape(columns, width)
    weight_col = jnp.sum(hop[:, at_weight:at_counts].astype(F32), axis=0)
    table = jnp.where(core == 0, token_grad, token_back)
    hop = spread(
        jnp.concatenate([table] + high_low(weight_col[:heads] + weight_col[heads:]), axis=0), COL
    )
    table = hop[:, :columns].reshape(total_tokens, width)
    weight = jnp.sum(hop[:, columns:].astype(F32), axis=0)
    of_row, rest = ids // tok_rows, ids % tok_rows
    back_ids = (rest // tile) * columns + of_row * tile + rest % tile
    picks = jnp.where(core == 0, ids, back_ids)
    slots = jnp.arange(total_tokens, dtype=jnp.int32)[None, :]
    picked = nn((picks[:, None] == slots).astype(BF), table).astype(BF)
    mine, other = picked[:n_atoms], lax.ppermute(picked[n_atoms:], "k", SWAP)
    grad_atom = atom_cot.astype(F32) + jnp.where(core == 0, mine, other).astype(F32)
    atom_out = (
        atom_single.astype(F32) + jnp.where(core == 0, other, mine).astype(F32)
    ).astype(BF)
    grad_bias = jnp.transpose(weight[:heads] + weight[heads:])
    return (atom_out, grad_atom, grad_bias)


def solution(mesh):
    rows, cols = mesh.devices.shape
    side = math.isqrt(cols)
    devices = mesh.devices.reshape(rows // 2, 2, side, side)
    everyone = ROW + COL
    return jax.shard_map(
        on_device,
        mesh=Mesh(devices, everyone),
        in_specs=(
            P(everyone, None),
            P(everyone),
            P(everyone, None),
            P(ROW, None),
            P(ROW, COL, None),
            P(),
            P(None, None, COL),
            P(),
            P(COL, None),
            P(),
        ),
        out_specs=(P(everyone, None), P(everyone, None), P()),
        check_vma=False,
    )
```

```python
import math

import jax
import jax.numpy as jnp
from jax import lax
from jax.experimental import pallas as pl
from jax.experimental.pallas import tpu as pltpu
from jax.sharding import Mesh
from jax.sharding import PartitionSpec as P

HD = 48


EPSILON = 1e-05
BF = jnp.bfloat16
F32 = jnp.float32


def nt(left, right):
    return lax.dot_general(left, right, (((1,), (1,)), ((), ())), preferred_element_type=F32)


def tn(left, right):
    return lax.dot_general(left, right, (((0,), (0,)), ((), ())), preferred_element_type=F32)


def nn(left, right):
    return jnp.dot(left, right, preferred_element_type=F32)


def exchange(blocks, axis):
    return lax.all_to_all(blocks, axis, split_axis=0, concat_axis=0, tiled=True)


def spread(block, axis):
    return exchange(jnp.broadcast_to(block[None], (lax.axis_size(axis),) + block.shape), axis)


def after(value, *others):
    return lax.optimization_barrier((value,) + others)[0]


def high_low(value):
    high = value.astype(BF)
    return [high, (value - high.astype(F32)).astype(BF)]


def norm_kernel(
    at, cond0, cond1, cond2, cond3, cond4, cond5, cond6, cond7, pooled_ref, pooled_other, wt_ref,
    wpool_ref, normed_ref, inv_ref, kv_ref, q_ref, qt_ref,
):
    cols, half, _ = normed_ref.shape
    conds = (cond0, cond1, cond2, cond3, cond4, cond5, cond6, cond7)
    for step in range(cols // 2):
        at_z = jnp.bitwise_xor(at[2], step // 2)
        b = 2 * at_z + jnp.bitwise_xor(at[3], step % 2)
        pools = pooled_other if step % 2 else pooled_ref
        single = conds[step][...].astype(F32) + nn(pools[at_z], wpool_ref[...])
        center = single - jnp.mean(single, axis=-1, keepdims=True)
        inverse = lax.rsqrt(jnp.mean(center * center, axis=-1, keepdims=True) + EPSILON)
        normed = (center * inverse).astype(BF)
        kv = nt(wt_ref[HD:], normed).astype(BF)
        for i in range(2):
            part = slice(i * half, (i + 1) * half)
            normed_ref[2 * b + i] = normed[part]
            inv_ref[2 * b + i] = inverse[part]
            kv_ref[2 * b + i] = kv[:, part]
        if step == 0:
            q_ref[...] = nt(normed, wt_ref[:HD]).astype(BF)
            qt_ref[...] = nt(wt_ref[:HD], normed).astype(BF)


def attend_kernel(
    q_ref, qt_ref, kv_ref, bias_ref, wout_ref, wdec_ref,
    out_ref, gkv_ref, gq_ref, att_ref, gout_ref, s_ref, g_ref,
):
    scale = 1.0 / math.sqrt(HD)
    blocks, tokens, columns = s_ref.shape
    half = columns // 2
    cols = 2 * blocks
    tile = tokens // cols

    def pair(ref, b, rows):
        return jnp.concatenate([ref[2 * b, rows], ref[2 * b + 1, rows]], axis=1)

    keys, values = slice(0, HD), slice(HD, 2 * HD)
    queries = q_ref[...]
    top = jnp.full((tokens, 1), -jnp.inf, F32)
    for b in range(blocks):
        bias = pair(bias_ref, b, slice(0, tokens))
        logits = nn(queries, pair(kv_ref, b, keys)) * scale + bias.astype(F32)
        s_ref[b] = logits
        top = jnp.maximum(top, jnp.max(logits, axis=-1, keepdims=True))
    total = jnp.zeros((tokens, 1), F32)
    for b in range(blocks):
        shifted = jnp.exp(s_ref[b] - top)
        s_ref[b] = shifted
        total = total + jnp.sum(shifted, axis=-1, keepdims=True)
    share = 1.0 / total

    cots = jnp.concatenate([bias_ref[c, tokens : tokens + tile] for c in range(cols)], axis=0)
    grad_out = nt(cots, wdec_ref[...])
    gout_ref[...] = grad_out
    grad_low = grad_out.astype(BF)
    grad_att = nt(grad_low, wout_ref[...]).astype(BF)
    grad_att_t = nt(wout_ref[...], grad_low).astype(BF)
    attended = jnp.zeros((tokens, HD), F32)
    delta = jnp.zeros((tokens, 1), F32)
    for b in range(blocks):
        probs = s_ref[b] * share
        s_ref[b] = probs
        block = pair(kv_ref, b, values)
        attended = attended + nt(probs.astype(BF), block)
        grad_probs = nn(grad_att, block)
        g_ref[b] = grad_probs
        delta = delta + jnp.sum(probs * grad_probs, axis=-1, keepdims=True)
    att_ref[...] = attended.astype(BF)

    grad_queries = jnp.zeros((tokens, HD), F32)
    for b in range(blocks):
        probs = s_ref[b]
        low = (probs * (g_ref[b] - delta)).astype(BF)
        out_ref[2 * b] = low[:, :half]
        out_ref[2 * b + 1] = low[:, half:]
        grad_queries = grad_queries + nt(low, pair(kv_ref, b, keys))
        grad_k = (nn(qt_ref[...], low) * scale).astype(BF)
        grad_v = nn(grad_att_t, probs.astype(BF)).astype(BF)
        gkv_ref[:, b * columns : (b + 1) * columns] = jnp.concatenate([grad_k, grad_v], axis=0)
    gq_ref[...] = (grad_queries * scale).astype(BF)


def token_grad_kernel(
    at, gkv_ref, gq_ref, att_ref, gout_ref, normed_ref, inv_ref, wt_ref, wpool_ref, wout_ref,
    wdec_ref, mine_ref, other_ref, back_ref, u_ref,
):
    cols, half, _ = normed_ref.shape
    tile, short = back_ref.shape[1], half // 2
    row, col, core = at[0], at[1], at[3]
    update = nn(att_ref[...], wout_ref[...]).astype(BF)
    back = nn(update, wdec_ref[...]).astype(BF)
    for c in range(cols):
        back_ref[c] = back[c * tile : (c + 1) * tile]
    for b in range(cols // 2):
        columns = slice(2 * b * half, 2 * (b + 1) * half)
        upstream = tn(gkv_ref[:, columns], wt_ref[HD:])
        u_ref[2 * b] = upstream[:half]
        u_ref[2 * b + 1] = upstream[half:]
    own = nn(gq_ref[...], wt_ref[:HD])
    u_ref[2 * row] += own[:half]
    u_ref[2 * row + 1] += own[half:]
    head = (col == 0).astype(F32)
    for c in range(cols):
        upstream = u_ref[c]
        normal = normed_ref[c].astype(F32)
        part = inv_ref[c] * (
            upstream
            - jnp.mean(upstream, axis=-1, keepdims=True)
            - normal * jnp.mean(upstream * normal, axis=-1, keepdims=True)
        )
        here = head * (row == c // 2).astype(F32)
        at_half = (c % 2) * half
        part = part + gout_ref[at_half : at_half + half] * here
        grad = nt(part.astype(BF), wpool_ref[...])
        mine_ref[c] = jnp.where(core == 0, grad[:short], grad[short:])
        other_ref[c] = jnp.where(core == 0, grad[short:], grad[:short]).astype(BF)


def call(body, outs, scratch, cost, *args, scalars=None):
    n_in, n_out, n_at = len(args), len(outs), int(scalars is not None)

    def kernel(*refs):
        at, refs = refs[:n_at], refs[n_at:]
        sources, results = refs[:n_in], refs[n_in : n_in + n_out]
        held = refs[n_in + n_out : 2 * (n_in + n_out)]
        sems, rest = refs[2 * (n_in + n_out)], refs[2 * (n_in + n_out) + 1 :]
        incoming = [
            pltpu.make_async_copy(src, dst, sems.at[i])
            for i, (src, dst) in enumerate(zip(sources, held[:n_in]))
        ]
        for copy in incoming:
            copy.start()
        for copy in incoming:
            copy.wait()
        body(*at, *held, *rest)
        outgoing = [
            pltpu.make_async_copy(src, dst, sems.at[n_in + i])
            for i, (src, dst) in enumerate(zip(held[n_in:], results))
        ]
        for copy in outgoing:
            copy.start()
        for copy in outgoing:
            copy.wait()

    anywhere = pl.BlockSpec(memory_space=pl.ANY)
    specs = [pl.BlockSpec(memory_space=pltpu.SMEM)] * n_at + [anywhere] * n_in
    return pl.pallas_call(
        kernel,
        in_specs=specs,
        out_specs=[anywhere] * n_out,
        out_shape=[jax.ShapeDtypeStruct(*out) for out in outs],
        scratch_shapes=[pltpu.VMEM(arg.shape, arg.dtype) for arg in args]
        + [pltpu.VMEM(*out) for out in outs]
        + [pltpu.SemaphoreType.DMA((n_in + n_out,))]
        + [pltpu.VMEM(*item) for item in scratch],
        compiler_params=pltpu.CompilerParams(vmem_limit_bytes=56 * 2**20),
        cost_estimate=pl.CostEstimate(
            flops=cost, bytes_accessed=8 * 2**20, transcendentals=2**19
        ),
    )(*([scalars] * n_at), *args)


ROW, COL, SAME_CORE = ("z", "k"), ("y", "x"), ("z", "y", "x")
SWAP = [(0, 1), (1, 0)]


def turn(value, axis, by):
    size = lax.axis_size(axis)
    return lax.ppermute(value, axis, [(i, i ^ by) for i in range(size)])


def take(value, start, size, axis=0):
    return lax.dynamic_slice_in_dim(value, start, size, axis)


def on_device(
    atom_single, atom_token, atom_cot, token_cond, pair, w_pool, w_qkv, w_bias, w_out, w_dec
):
    side = lax.axis_size("x")
    rows, cols = lax.axis_size("z") * 2, lax.axis_size("y") * side
    z, core, y, x = [lax.axis_index(name) for name in ("z", "k", "y", "x")]
    row, col = z * 2 + core, y * side + x
    tok_rows = token_cond.shape[0]
    total_tokens = tok_rows * rows
    n_atoms, width = atom_single.shape
    tile, columns = tok_rows // cols, total_tokens // cols
    peers = rows * cols // 2
    at = jnp.stack([row, col, z, core]).astype(jnp.int32)
    w_t = jnp.transpose(w_qkv, (0, 2, 1)).reshape(3 * HD, -1)

    ids = jnp.concatenate([atom_token, lax.ppermute(atom_token, "k", SWAP)])
    singles = jnp.concatenate([atom_single, lax.ppermute(atom_single, "k", SWAP)], axis=0)
    cots = jnp.concatenate([atom_cot, lax.ppermute(atom_cot, "k", SWAP)], axis=0)
    slots = jnp.arange(total_tokens // 2, dtype=jnp.int32)
    slots = (slots // tok_rows * 2 + core) * tok_rows + slots % tok_rows
    onehot = (slots[:, None] == ids[None, :]).astype(BF)
    with_ones = jnp.concatenate([singles, cots, jnp.ones_like(singles)], axis=1)
    partial = nn(onehot, with_ones).reshape(peers, tile, 3 * width)
    place = jnp.eye(tile, width, dtype=F32)
    partial_counts = jnp.sum(partial[:, :, 2 * width :] * place, axis=1, keepdims=True)
    to_tiles = jnp.concatenate(
        [
            partial[:, :, :width].astype(BF),
            partial[:, :, width : 2 * width].astype(BF),
            jnp.pad(partial_counts.astype(BF), ((0, 0), (0, 7), (0, 0))),
        ],
        axis=1,
    )

    bias = jnp.einsum("ijc,ch->hij", pair, w_bias, preferred_element_type=F32).astype(BF)
    from_all = exchange(to_tiles, SAME_CORE)
    from_all = after(from_all, bias)
    sums = jnp.sum(from_all.astype(F32), axis=0)
    tile_counts = jnp.sum(sums[2 * tile : 2 * tile + 1] * place, axis=1, keepdims=True)
    pooled_tile = (sums[:tile] / tile_counts).astype(BF)
    lanes = jnp.arange(width, dtype=jnp.int32)[None]
    seat = jnp.arange(tile, dtype=jnp.int32)[:, None] + tile * (col % (cols // 2))
    count_row = jnp.sum(jnp.where(lanes == seat, tile_counts, 0.0), axis=0, keepdims=True)
    count_row = jnp.where(jnp.arange(8)[:, None] == col // (cols // 2), count_row, 0.0)
    count_row = jnp.pad(count_row[:2], ((0, tile - 2), (0, 0)))
    shared = jnp.concatenate([sums[tile : 2 * tile], count_row], axis=0).astype(BF)
    shared = jnp.broadcast_to(shared[None], (cols, 2 * tile, width))
    pooled = spread(pooled_tile, SAME_CORE)
    late_cond = after(token_cond, bias)
    pieces = [turn(late_cond, "z", d) for d in (1, 2, 3)]
    pooled = pooled.reshape(rows // 2, tok_rows, width)
    to_col = after(jnp.concatenate([bias, shared], axis=1), pooled, *pieces)
    bias_cot = exchange(to_col, COL)
    conds = []
    for piece in [token_cond] + pieces:
        piece = after(piece, to_col)
        conds += [piece, lax.ppermute(piece, "k", SWAP)]
    other_pooled = lax.ppermute(pooled, "k", SWAP)
    single_tile = take(token_cond, col * tile, tile).astype(F32) + nn(pooled_tile, w_pool)
    tile_base = nn(single_tile.astype(BF), w_dec)
    features = w_t.shape[1]
    normed, inverse, kv, queries, queries_t = call(
        norm_kernel,
        [
            ((cols, columns, features), BF),
            ((cols, columns, 1), F32),
            ((cols, 2 * HD, columns), BF),
            ((tok_rows, HD), BF),
            ((HD, tok_rows), BF),
        ],
        [], 10**9, *conds, pooled, other_pooled, w_t, w_pool, scalars=at,
    )
    bias_cot = after(bias_cot, kv, tile_base)
    row_counts = jnp.sum(bias_cot[:, tok_rows + tile : tok_rows + tile + 2].astype(F32), axis=0)
    block_counts = jnp.where(row == col // 2, take(row_counts, col % 2, 1), 0.0).astype(BF)

    spread_logits = (rows, tok_rows, 2 * columns)
    grad_logits, grad_kv, grad_queries, attended, grad_out = call(
        attend_kernel,
        [
            ((cols, tok_rows, columns), BF),
            ((2 * HD, total_tokens), BF),
            ((tok_rows, HD), BF),
            ((tok_rows, HD), BF),
            ((tok_rows, features), F32),
        ],
        [(spread_logits, F32), (spread_logits, F32)],
        2 * 10**9, queries, queries_t, kv, bias_cot, w_out, w_dec,
    )
    bias_back = exchange(grad_logits, COL)
    mine, other, back = call(
        token_grad_kernel,
        [
            ((cols, columns // 2, width), F32),
            ((cols, columns // 2, width), BF),
            ((cols, tile, width), BF),
        ],
        [((cols, columns, features), F32)],
        10**9,
        grad_kv, grad_queries, attended, grad_out, normed, inverse, w_t, w_pool, w_out, w_dec,
        scalars=at,
    )
    grad_part = (mine + lax.ppermute(other, "k", SWAP).astype(F32)).astype(BF)
    to_col = jnp.concatenate([grad_part, back], axis=1)
    bias_back = after(bias_back, to_col)
    hop = exchange(after(to_col, bias_back), COL)
    weight_part = jnp.einsum("ijc,hij->hc", pair, bias_back, preferred_element_type=F32)
    hop = after(hop, weight_part)
    block_counts = block_counts + lax.ppermute(block_counts, "k", SWAP)
    rest = jnp.sum(hop.astype(F32), axis=0)
    heads = weight_part.shape[0]
    hop = spread(
        jnp.concatenate(
            [rest[: columns // 2].astype(BF), (tile_base + rest[columns // 2 :]).astype(BF)]
            + high_low(weight_part)
            + [jnp.pad(block_counts, ((0, 15), (0, 0)))],
            axis=0,
        ),
        "z",
    )
    at_back = columns // 2
    at_weight = at_back + tile
    at_counts = at_weight + 2 * heads
    count_row = jnp.sum(hop[:, at_counts : at_counts + 1].astype(F32), axis=0)
    seats = core * at_back + jnp.arange(at_back, dtype=jnp.int32)[:, None]
    own_counts = jnp.sum(jnp.where(lanes == seats, count_row, 0.0), axis=1, keepdims=True)
    token_grad = (jnp.sum(hop[:, :at_back].astype(F32), axis=0) / own_counts).astype(BF)
    token_back = hop[:, at_back:at_weight].reshape(at_back, width)
    weight_col = jnp.sum(hop[:, at_weight:at_counts].astype(F32), axis=0)
    hop = spread(
        jnp.concatenate(
            [token_grad, token_back] + high_low(weight_col[:heads] + weight_col[heads:]), axis=0
        ),
        COL,
    )
    weight = jnp.sum(hop[:, columns:].astype(F32), axis=0)
    weight = weight[:heads] + weight[heads:]
    grad_table = hop[:, :at_back].reshape(cols * at_back, width)
    back_table = hop[:, at_back:columns].reshape(cols * at_back, width)
    slots = jnp.arange(cols * at_back, dtype=jnp.int32)[None, :]
    of_row, rest = ids // tok_rows, ids % tok_rows
    grad_ids = ids // columns * at_back + ids % at_back
    grad_ids = jnp.where(ids % columns // at_back == core, grad_ids, -1)
    back_ids = rest // tile * at_back + of_row // 2 * tile + rest % tile
    back_ids = jnp.where(of_row % 2 == core, back_ids, -1)
    picked = jnp.concatenate(
        [
            nn((back_ids[:, None] == slots).astype(BF), back_table).astype(BF),
            nn((grad_ids[:, None] == slots).astype(BF), grad_table).astype(BF),
        ],
        axis=1,
    )
    other = lax.ppermute(picked[n_atoms:], "k", SWAP)
    picked = picked[:n_atoms].astype(F32) + other.astype(F32)
    atom_out = (atom_single.astype(F32) + picked[:, :width]).astype(BF)
    grad_atom = atom_cot.astype(F32) + picked[:, width:]
    grad_bias = jnp.transpose(weight + lax.ppermute(weight, "k", SWAP))
    return (atom_out, grad_atom, grad_bias)


def solution(mesh):
    rows, cols = mesh.devices.shape
    side = math.isqrt(cols)
    devices = mesh.devices.reshape(rows // 2, 2, side, side)
    everyone = ROW + COL
    return jax.shard_map(
        on_device,
        mesh=Mesh(devices, everyone),
        in_specs=(
            P(everyone, None),
            P(everyone),
            P(everyone, None),
            P(ROW, None),
            P(ROW, COL, None),
            P(),
            P(None, None, COL),
            P(),
            P(COL, None),
            P(),
        ),
        out_specs=(P(everyone, None), P(everyone, None), P()),
        check_vma=False,
    )
```

```python
import math

import jax
import jax.numpy as jnp
from jax import lax
from jax.experimental import pallas as pl
from jax.experimental.pallas import tpu as pltpu
from jax.sharding import Mesh
from jax.sharding import PartitionSpec as P

HD = 48


EPSILON = 1e-05
BF = jnp.bfloat16
F32 = jnp.float32


def nt(left, right):
    return lax.dot_general(left, right, (((1,), (1,)), ((), ())), preferred_element_type=F32)


def tn(left, right):
    return lax.dot_general(left, right, (((0,), (0,)), ((), ())), preferred_element_type=F32)


def nn(left, right):
    return jnp.dot(left, right, preferred_element_type=F32)


def exchange(blocks, axis):
    return lax.all_to_all(blocks, axis, split_axis=0, concat_axis=0, tiled=True)


def spread(block, axis):
    return exchange(jnp.broadcast_to(block[None], (lax.axis_size(axis),) + block.shape), axis)


def after(value, *others):
    return lax.optimization_barrier((value,) + others)[0]


def high_low(value):
    high = value.astype(BF)
    return [high, (value - high.astype(F32)).astype(BF)]


def norm_kernel(
    at, cond0, cond1, cond2, cond3, cond4, cond5, cond6, cond7, pooled_ref, pooled_other, wt_ref,
    wpool_ref, normed_ref, inv_ref, kv_ref, q_ref, qt_ref,
):
    cols, half, _ = normed_ref.shape
    conds = (cond0, cond1, cond2, cond3, cond4, cond5, cond6, cond7)
    for step in range(cols // 2):
        at_z = jnp.bitwise_xor(at[2], step // 2)
        b = 2 * at_z + jnp.bitwise_xor(at[3], step % 2)
        pools = pooled_other if step % 2 else pooled_ref
        single = conds[step][...].astype(F32) + nn(pools[at_z], wpool_ref[...])
        center = single - jnp.mean(single, axis=-1, keepdims=True)
        inverse = lax.rsqrt(jnp.mean(center * center, axis=-1, keepdims=True) + EPSILON)
        normed = (center * inverse).astype(BF)
        kv = nt(wt_ref[HD:], normed).astype(BF)
        for i in range(2):
            part = slice(i * half, (i + 1) * half)
            normed_ref[2 * b + i] = normed[part]
            inv_ref[2 * b + i] = inverse[part]
            kv_ref[2 * b + i] = kv[:, part]
        if step == 0:
            q_ref[...] = nt(normed, wt_ref[:HD]).astype(BF)
            qt_ref[...] = nt(wt_ref[:HD], normed).astype(BF)


def attend_kernel(
    q_ref, qt_ref, kv_ref, bias_ref, wout_ref, wdec_ref,
    out_ref, gkv_ref, gq_ref, att_ref, gout_ref, s_ref, g_ref,
):
    scale = 1.0 / math.sqrt(HD)
    blocks, tokens, columns = s_ref.shape
    half = columns // 2
    cols = 2 * blocks
    tile = tokens // cols

    def pair(ref, b, rows):
        return jnp.concatenate([ref[2 * b, rows], ref[2 * b + 1, rows]], axis=1)

    keys, values = slice(0, HD), slice(HD, 2 * HD)
    queries = q_ref[...]
    top = jnp.full((tokens, 1), -jnp.inf, F32)
    for b in range(blocks):
        bias = pair(bias_ref, b, slice(0, tokens))
        logits = nn(queries, pair(kv_ref, b, keys)) * scale + bias.astype(F32)
        s_ref[b] = logits
        top = jnp.maximum(top, jnp.max(logits, axis=-1, keepdims=True))
    total = jnp.zeros((tokens, 1), F32)
    for b in range(blocks):
        shifted = jnp.exp(s_ref[b] - top)
        s_ref[b] = shifted
        total = total + jnp.sum(shifted, axis=-1, keepdims=True)
    share = 1.0 / total

    cots = jnp.concatenate([bias_ref[c, tokens : tokens + tile] for c in range(cols)], axis=0)
    grad_out = nt(cots, wdec_ref[...])
    gout_ref[...] = grad_out
    grad_low = grad_out.astype(BF)
    grad_att = nt(grad_low, wout_ref[...]).astype(BF)
    grad_att_t = nt(wout_ref[...], grad_low).astype(BF)
    attended = jnp.zeros((tokens, HD), F32)
    delta = jnp.zeros((tokens, 1), F32)
    for b in range(blocks):
        probs = s_ref[b] * share
        s_ref[b] = probs
        block = pair(kv_ref, b, values)
        attended = attended + nt(probs.astype(BF), block)
        grad_probs = nn(grad_att, block)
        g_ref[b] = grad_probs
        delta = delta + jnp.sum(probs * grad_probs, axis=-1, keepdims=True)
    att_ref[...] = attended.astype(BF)

    grad_queries = jnp.zeros((tokens, HD), F32)
    for b in range(blocks):
        probs = s_ref[b]
        low = (probs * (g_ref[b] - delta)).astype(BF)
        out_ref[2 * b] = low[:, :half]
        out_ref[2 * b + 1] = low[:, half:]
        grad_queries = grad_queries + nt(low, pair(kv_ref, b, keys))
        grad_k = (nn(qt_ref[...], low) * scale).astype(BF)
        grad_v = nn(grad_att_t, probs.astype(BF)).astype(BF)
        gkv_ref[:, b * columns : (b + 1) * columns] = jnp.concatenate([grad_k, grad_v], axis=0)
    gq_ref[...] = (grad_queries * scale).astype(BF)


def token_grad_kernel(
    at, gkv_ref, gq_ref, att_ref, gout_ref, normed_ref, inv_ref, wt_ref, wpool_ref, wout_ref,
    wdec_ref, mine_ref, other_ref, back_ref, u_ref,
):
    cols, half, _ = normed_ref.shape
    tile, short = back_ref.shape[1], half // 2
    row, col, core = at[0], at[1], at[3]
    update = nn(att_ref[...], wout_ref[...]).astype(BF)
    back = nn(update, wdec_ref[...]).astype(BF)
    for c in range(cols):
        back_ref[c] = back[c * tile : (c + 1) * tile]
    for b in range(cols // 2):
        columns = slice(2 * b * half, 2 * (b + 1) * half)
        upstream = tn(gkv_ref[:, columns], wt_ref[HD:])
        u_ref[2 * b] = upstream[:half]
        u_ref[2 * b + 1] = upstream[half:]
    own = nn(gq_ref[...], wt_ref[:HD])
    u_ref[2 * row] += own[:half]
    u_ref[2 * row + 1] += own[half:]
    head = (col == 0).astype(F32)
    for c in range(cols):
        upstream = u_ref[c]
        normal = normed_ref[c].astype(F32)
        part = inv_ref[c] * (
            upstream
            - jnp.mean(upstream, axis=-1, keepdims=True)
            - normal * jnp.mean(upstream * normal, axis=-1, keepdims=True)
        )
        here = head * (row == c // 2).astype(F32)
        at_half = (c % 2) * half
        part = part + gout_ref[at_half : at_half + half] * here
        grad = nt(part.astype(BF), wpool_ref[...])
        mine_ref[c] = jnp.where(core == 0, grad[:short], grad[short:])
        other_ref[c] = jnp.where(core == 0, grad[short:], grad[:short]).astype(BF)


def call(body, outs, scratch, cost, *args, scalars=None):
    n_in, n_out, n_at = len(args), len(outs), int(scalars is not None)

    def kernel(*refs):
        at, refs = refs[:n_at], refs[n_at:]
        sources, results = refs[:n_in], refs[n_in : n_in + n_out]
        held = refs[n_in + n_out : 2 * (n_in + n_out)]
        sems, rest = refs[2 * (n_in + n_out)], refs[2 * (n_in + n_out) + 1 :]
        incoming = [
            pltpu.make_async_copy(src, dst, sems.at[i])
            for i, (src, dst) in enumerate(zip(sources, held[:n_in]))
        ]
        for copy in incoming:
            copy.start()
        for copy in incoming:
            copy.wait()
        body(*at, *held, *rest)
        outgoing = [
            pltpu.make_async_copy(src, dst, sems.at[n_in + i])
            for i, (src, dst) in enumerate(zip(held[n_in:], results))
        ]
        for copy in outgoing:
            copy.start()
        for copy in outgoing:
            copy.wait()

    anywhere = pl.BlockSpec(memory_space=pl.ANY)
    specs = [pl.BlockSpec(memory_space=pltpu.SMEM)] * n_at + [anywhere] * n_in
    return pl.pallas_call(
        kernel,
        in_specs=specs,
        out_specs=[anywhere] * n_out,
        out_shape=[jax.ShapeDtypeStruct(*out) for out in outs],
        scratch_shapes=[pltpu.VMEM(arg.shape, arg.dtype) for arg in args]
        + [pltpu.VMEM(*out) for out in outs]
        + [pltpu.SemaphoreType.DMA((n_in + n_out,))]
        + [pltpu.VMEM(*item) for item in scratch],
        compiler_params=pltpu.CompilerParams(vmem_limit_bytes=56 * 2**20),
        cost_estimate=pl.CostEstimate(
            flops=cost, bytes_accessed=8 * 2**20, transcendentals=2**19
        ),
    )(*([scalars] * n_at), *args)


ROW, COL, SAME_CORE = ("z", "k"), ("y", "x"), ("z", "y", "x")
SWAP = [(0, 1), (1, 0)]


def turn(value, axis, by):
    size = lax.axis_size(axis)
    return lax.ppermute(value, axis, [(i, i ^ by) for i in range(size)])


def take(value, start, size, axis=0):
    return lax.dynamic_slice_in_dim(value, start, size, axis)


def on_device(
    atom_single, atom_token, atom_cot, token_cond, pair, w_pool, w_qkv, w_bias, w_out, w_dec
):
    side = lax.axis_size("x")
    rows, cols = lax.axis_size("z") * 2, lax.axis_size("y") * side
    z, core, y, x = [lax.axis_index(name) for name in ("z", "k", "y", "x")]
    row, col = z * 2 + core, y * side + x
    tok_rows = token_cond.shape[0]
    total_tokens = tok_rows * rows
    n_atoms, width = atom_single.shape
    tile, columns = tok_rows // cols, total_tokens // cols
    peers = rows * cols // 2
    at = jnp.stack([row, col, z, core]).astype(jnp.int32)
    w_t = jnp.transpose(w_qkv, (0, 2, 1)).reshape(3 * HD, -1)

    ids = jnp.concatenate([atom_token, lax.ppermute(atom_token, "k", SWAP)])
    singles = jnp.concatenate([atom_single, lax.ppermute(atom_single, "k", SWAP)], axis=0)
    cots = jnp.concatenate([atom_cot, lax.ppermute(atom_cot, "k", SWAP)], axis=0)
    slots = jnp.arange(total_tokens // 2, dtype=jnp.int32)
    slots = (slots // tok_rows * 2 + core) * tok_rows + slots % tok_rows
    onehot = (slots[:, None] == ids[None, :]).astype(BF)
    with_ones = jnp.concatenate([singles, cots, jnp.ones_like(singles)], axis=1)
    partial = nn(onehot, with_ones).reshape(peers, tile, 3 * width)
    place = jnp.eye(tile, width, dtype=F32)
    partial_counts = jnp.sum(partial[:, :, 2 * width :] * place, axis=1, keepdims=True)
    to_tiles = jnp.concatenate(
        [
            partial[:, :, :width].astype(BF),
            partial[:, :, width : 2 * width].astype(BF),
            jnp.pad(partial_counts.astype(BF), ((0, 0), (0, 7), (0, 0))),
        ],
        axis=1,
    )

    bias = jnp.einsum("ijc,ch->hij", pair, w_bias, preferred_element_type=F32).astype(BF)
    from_all = exchange(to_tiles, SAME_CORE)
    from_all = after(from_all, bias)
    sums = jnp.sum(from_all.astype(F32), axis=0)
    tile_counts = jnp.sum(sums[2 * tile : 2 * tile + 1] * place, axis=1, keepdims=True)
    pooled_tile = (sums[:tile] / tile_counts).astype(BF)
    lanes = jnp.arange(width, dtype=jnp.int32)[None]
    seat = jnp.arange(tile, dtype=jnp.int32)[:, None] + tile * (col % (cols // 2))
    count_row = jnp.sum(jnp.where(lanes == seat, tile_counts, 0.0), axis=0, keepdims=True)
    count_row = jnp.where(jnp.arange(8)[:, None] == col // (cols // 2), count_row, 0.0)
    count_row = jnp.pad(count_row[:2], ((0, tile - 2), (0, 0)))
    shared = jnp.concatenate([sums[tile : 2 * tile], count_row], axis=0).astype(BF)
    shared = jnp.broadcast_to(shared[None], (cols, 2 * tile, width))
    pooled = spread(pooled_tile, SAME_CORE)
    late_cond = after(token_cond, bias)
    pieces = [turn(late_cond, "z", d) for d in (1, 2, 3)]
    pooled = pooled.reshape(rows // 2, tok_rows, width)
    to_col = after(jnp.concatenate([bias, shared], axis=1), pooled, *pieces)
    bias_cot = exchange(to_col, COL)
    conds = []
    for piece in [token_cond] + pieces:
        piece = after(piece, to_col)
        conds += [piece, lax.ppermute(piece, "k", SWAP)]
    other_pooled = lax.ppermute(pooled, "k", SWAP)
    single_tile = take(token_cond, col * tile, tile).astype(F32) + nn(pooled_tile, w_pool)
    tile_base = nn(single_tile.astype(BF), w_dec)
    features = w_t.shape[1]
    normed, inverse, kv, queries, queries_t = call(
        norm_kernel,
        [
            ((cols, columns, features), BF),
            ((cols, columns, 1), F32),
            ((cols, 2 * HD, columns), BF),
            ((tok_rows, HD), BF),
            ((HD, tok_rows), BF),
        ],
        [], 10**9, *conds, pooled, other_pooled, w_t, w_pool, scalars=at,
    )
    bias_cot = after(bias_cot, kv, tile_base)
    row_counts = jnp.sum(bias_cot[:, tok_rows + tile : tok_rows + tile + 2].astype(F32), axis=0)
    block_counts = jnp.where(row == col // 2, take(row_counts, col % 2, 1), 0.0).astype(BF)

    spread_logits = (rows, tok_rows, 2 * columns)
    grad_logits, grad_kv, grad_queries, attended, grad_out = call(
        attend_kernel,
        [
            ((cols, tok_rows, columns), BF),
            ((2 * HD, total_tokens), BF),
            ((tok_rows, HD), BF),
            ((tok_rows, HD), BF),
            ((tok_rows, features), F32),
        ],
        [(spread_logits, F32), (spread_logits, F32)],
        2 * 10**9, queries, queries_t, kv, bias_cot, w_out, w_dec,
    )
    bias_back = exchange(grad_logits, COL)
    mine, other, back = call(
        token_grad_kernel,
        [
            ((cols, columns // 2, width), F32),
            ((cols, columns // 2, width), BF),
            ((cols, tile, width), BF),
        ],
        [((cols, columns, features), F32)],
        10**9,
        grad_kv, grad_queries, attended, grad_out, normed, inverse, w_t, w_pool, w_out, w_dec,
        scalars=at,
    )
    grad_part = (mine + lax.ppermute(other, "k", SWAP).astype(F32)).astype(BF)
    to_col = jnp.concatenate([grad_part, back], axis=1)
    bias_back = after(bias_back, to_col)
    hop = exchange(after(to_col, bias_back), COL)
    weight_part = jnp.einsum("ijc,hij->hc", pair, bias_back, preferred_element_type=F32)
    hop = after(hop, weight_part)
    block_counts = block_counts + lax.ppermute(block_counts, "k", SWAP)
    rest = jnp.sum(hop.astype(F32), axis=0)
    heads = weight_part.shape[0]
    to_z = jnp.concatenate(
        [rest[: columns // 2].astype(BF), (tile_base + rest[columns // 2 :]).astype(BF)]
        + high_low(weight_part)
        + [jnp.pad(block_counts, ((0, 15), (0, 0)))],
        axis=0,
    )
    hop = jnp.stack([to_z] + [turn(to_z, "z", d) for d in (1, 2, 3)])
    at_back = columns // 2
    at_weight = at_back + tile
    at_counts = at_weight + 2 * heads
    count_row = jnp.sum(hop[:, at_counts : at_counts + 1].astype(F32), axis=0)
    seats = core * at_back + jnp.arange(at_back, dtype=jnp.int32)[:, None]
    own_counts = jnp.sum(jnp.where(lanes == seats, count_row, 0.0), axis=1, keepdims=True)
    token_grad = (jnp.sum(hop[:, :at_back].astype(F32), axis=0) / own_counts).astype(BF)
    token_back = hop[:, at_back:at_weight].reshape(at_back, width)
    weight_col = jnp.sum(hop[:, at_weight:at_counts].astype(F32), axis=0)
    hop = spread(
        jnp.concatenate(
            [token_grad, token_back] + high_low(weight_col[:heads] + weight_col[heads:]), axis=0
        ),
        COL,
    )
    weight = jnp.sum(hop[:, columns:].astype(F32), axis=0)
    weight = weight[:heads] + weight[heads:]
    grad_table = hop[:, :at_back].reshape(cols * at_back, width)
    back_table = hop[:, at_back:columns].reshape(cols * at_back, width)
    slots = jnp.arange(cols * at_back, dtype=jnp.int32)[None, :]
    of_row, rest = ids // tok_rows, ids % tok_rows
    grad_ids = ids // columns * at_back + ids % at_back
    grad_ids = jnp.where(ids % columns // at_back == core, grad_ids, -1)
    back_ids = rest // tile * at_back + jnp.bitwise_xor(of_row // 2, z) * tile + rest % tile
    back_ids = jnp.where(of_row % 2 == core, back_ids, -1)
    backs = nn((back_ids[:, None] == slots).astype(BF), back_table).astype(BF)
    grads = nn((grad_ids[:, None] == slots).astype(BF), grad_table).astype(BF)
    other_backs = lax.ppermute(backs[n_atoms:], "k", SWAP)
    other_grads = lax.ppermute(grads[n_atoms:], "k", SWAP)
    backs = backs[:n_atoms].astype(F32) + other_backs.astype(F32)
    grads = grads[:n_atoms].astype(F32) + other_grads.astype(F32)
    atom_out = (atom_single.astype(F32) + backs).astype(BF)
    grad_atom = atom_cot.astype(F32) + grads
    grad_bias = jnp.transpose(weight + lax.ppermute(weight, "k", SWAP))
    return (atom_out, grad_atom, grad_bias)


def solution(mesh):
    rows, cols = mesh.devices.shape
    side = math.isqrt(cols)
    devices = mesh.devices.reshape(rows // 2, 2, side, side)
    everyone = ROW + COL
    return jax.shard_map(
        on_device,
        mesh=Mesh(devices, everyone),
        in_specs=(
            P(everyone, None),
            P(everyone),
            P(everyone, None),
            P(ROW, None),
            P(ROW, COL, None),
            P(),
            P(None, None, COL),
            P(),
            P(COL, None),
            P(),
        ),
        out_specs=(P(everyone, None), P(everyone, None), P()),
        check_vma=False,
    )
```

```python
import math

import jax
import jax.numpy as jnp
from jax import lax
from jax.experimental import pallas as pl
from jax.experimental.pallas import tpu as pltpu
from jax.sharding import Mesh
from jax.sharding import PartitionSpec as P

HD = 48


EPSILON = 1e-05
BF = jnp.bfloat16
F32 = jnp.float32


def nt(left, right):
    return lax.dot_general(left, right, (((1,), (1,)), ((), ())), preferred_element_type=F32)


def tn(left, right):
    return lax.dot_general(left, right, (((0,), (0,)), ((), ())), preferred_element_type=F32)


def nn(left, right):
    return jnp.dot(left, right, preferred_element_type=F32)


def exchange(blocks, axis):
    return lax.all_to_all(blocks, axis, split_axis=0, concat_axis=0, tiled=True)


def spread(block, axis):
    return exchange(jnp.broadcast_to(block[None], (lax.axis_size(axis),) + block.shape), axis)


def after(value, *others):
    return lax.optimization_barrier((value,) + others)[0]


def high_low(value):
    high = value.astype(BF)
    return [high, (value - high.astype(F32)).astype(BF)]


def norm_kernel(
    at, cond0, cond1, cond2, cond3, cond4, cond5, cond6, cond7, pooled_ref, pooled_other, wt_ref,
    wpool_ref, normed_ref, inv_ref, kv_ref, q_ref, qt_ref,
):
    cols, half, _ = normed_ref.shape
    conds = (cond0, cond1, cond2, cond3, cond4, cond5, cond6, cond7)
    for step in range(cols // 2):
        at_z = jnp.bitwise_xor(at[2], step // 2)
        b = 2 * at_z + jnp.bitwise_xor(at[3], step % 2)
        pools = pooled_other if step % 2 else pooled_ref
        single = conds[step][...].astype(F32) + nn(pools[at_z], wpool_ref[...])
        center = single - jnp.mean(single, axis=-1, keepdims=True)
        inverse = lax.rsqrt(jnp.mean(center * center, axis=-1, keepdims=True) + EPSILON)
        normed = (center * inverse).astype(BF)
        kv = nt(wt_ref[HD:], normed).astype(BF)
        for i in range(2):
            part = slice(i * half, (i + 1) * half)
            normed_ref[2 * b + i] = normed[part]
            inv_ref[2 * b + i] = inverse[part]
            kv_ref[2 * b + i] = kv[:, part]
        if step == 0:
            q_ref[...] = nt(normed, wt_ref[:HD]).astype(BF)
            qt_ref[...] = nt(wt_ref[:HD], normed).astype(BF)


def attend_kernel(
    q_ref, qt_ref, kv_ref, bias_ref, wout_ref, wdec_ref,
    out_ref, gkv_ref, gq_ref, att_ref, gout_ref, s_ref, g_ref,
):
    scale = 1.0 / math.sqrt(HD)
    blocks, tokens, columns = s_ref.shape
    half = columns // 2
    cols = 2 * blocks
    tile = tokens // cols

    def pair(ref, b, rows):
        return jnp.concatenate([ref[2 * b, rows], ref[2 * b + 1, rows]], axis=1)

    keys, values = slice(0, HD), slice(HD, 2 * HD)
    queries = q_ref[...]
    top = jnp.full((tokens, 1), -jnp.inf, F32)
    for b in range(blocks):
        bias = pair(bias_ref, b, slice(0, tokens))
        logits = nn(queries, pair(kv_ref, b, keys)) * scale + bias.astype(F32)
        s_ref[b] = logits
        top = jnp.maximum(top, jnp.max(logits, axis=-1, keepdims=True))
    total = jnp.zeros((tokens, 1), F32)
    for b in range(blocks):
        shifted = jnp.exp(s_ref[b] - top)
        s_ref[b] = shifted
        total = total + jnp.sum(shifted, axis=-1, keepdims=True)
    share = 1.0 / total

    cots = jnp.concatenate([bias_ref[c, tokens : tokens + tile] for c in range(cols)], axis=0)
    grad_out = nt(cots, wdec_ref[...])
    gout_ref[...] = grad_out
    grad_low = grad_out.astype(BF)
    grad_att = nt(grad_low, wout_ref[...]).astype(BF)
    grad_att_t = nt(wout_ref[...], grad_low).astype(BF)
    attended = jnp.zeros((tokens, HD), F32)
    delta = jnp.zeros((tokens, 1), F32)
    for b in range(blocks):
        probs = s_ref[b] * share
        s_ref[b] = probs
        block = pair(kv_ref, b, values)
        attended = attended + nt(probs.astype(BF), block)
        grad_probs = nn(grad_att, block)
        g_ref[b] = grad_probs
        delta = delta + jnp.sum(probs * grad_probs, axis=-1, keepdims=True)
    att_ref[...] = attended.astype(BF)

    grad_queries = jnp.zeros((tokens, HD), F32)
    for b in range(blocks):
        probs = s_ref[b]
        low = (probs * (g_ref[b] - delta)).astype(BF)
        out_ref[2 * b] = low[:, :half]
        out_ref[2 * b + 1] = low[:, half:]
        grad_queries = grad_queries + nt(low, pair(kv_ref, b, keys))
        grad_k = (nn(qt_ref[...], low) * scale).astype(BF)
        grad_v = nn(grad_att_t, probs.astype(BF)).astype(BF)
        gkv_ref[:, b * columns : (b + 1) * columns] = jnp.concatenate([grad_k, grad_v], axis=0)
    gq_ref[...] = (grad_queries * scale).astype(BF)


def token_grad_kernel(
    at, gkv_ref, gq_ref, att_ref, gout_ref, normed_ref, inv_ref, wt_ref, wpool_ref, wout_ref,
    wdec_ref, mine_ref, other_ref, back_ref, u_ref,
):
    cols, half, _ = normed_ref.shape
    tile, short = back_ref.shape[1], half // 2
    row, col, core = at[0], at[1], at[3]
    update = nn(att_ref[...], wout_ref[...]).astype(BF)
    back = nn(update, wdec_ref[...]).astype(BF)
    for c in range(cols):
        back_ref[c] = back[c * tile : (c + 1) * tile]
    for b in range(cols // 2):
        columns = slice(2 * b * half, 2 * (b + 1) * half)
        upstream = tn(gkv_ref[:, columns], wt_ref[HD:])
        u_ref[2 * b] = upstream[:half]
        u_ref[2 * b + 1] = upstream[half:]
    own = nn(gq_ref[...], wt_ref[:HD])
    u_ref[2 * row] += own[:half]
    u_ref[2 * row + 1] += own[half:]
    head = (col == 0).astype(F32)
    for c in range(cols):
        upstream = u_ref[c]
        normal = normed_ref[c].astype(F32)
        part = inv_ref[c] * (
            upstream
            - jnp.mean(upstream, axis=-1, keepdims=True)
            - normal * jnp.mean(upstream * normal, axis=-1, keepdims=True)
        )
        here = head * (row == c // 2).astype(F32)
        at_half = (c % 2) * half
        part = part + gout_ref[at_half : at_half + half] * here
        grad = nt(part.astype(BF), wpool_ref[...])
        mine_ref[c] = jnp.where(core == 0, grad[:short], grad[short:])
        other_ref[c] = jnp.where(core == 0, grad[short:], grad[:short]).astype(BF)


def call(body, outs, scratch, cost, *args, scalars=None):
    n_in, n_out, n_at = len(args), len(outs), int(scalars is not None)

    def kernel(*refs):
        at, refs = refs[:n_at], refs[n_at:]
        sources, results = refs[:n_in], refs[n_in : n_in + n_out]
        held = refs[n_in + n_out : 2 * (n_in + n_out)]
        sems, rest = refs[2 * (n_in + n_out)], refs[2 * (n_in + n_out) + 1 :]
        incoming = [
            pltpu.make_async_copy(src, dst, sems.at[i])
            for i, (src, dst) in enumerate(zip(sources, held[:n_in]))
        ]
        for copy in incoming:
            copy.start()
        for copy in incoming:
            copy.wait()
        body(*at, *held, *rest)
        outgoing = [
            pltpu.make_async_copy(src, dst, sems.at[n_in + i])
            for i, (src, dst) in enumerate(zip(held[n_in:], results))
        ]
        for copy in outgoing:
            copy.start()
        for copy in outgoing:
            copy.wait()

    anywhere = pl.BlockSpec(memory_space=pl.ANY)
    specs = [pl.BlockSpec(memory_space=pltpu.SMEM)] * n_at + [anywhere] * n_in
    return pl.pallas_call(
        kernel,
        in_specs=specs,
        out_specs=[anywhere] * n_out,
        out_shape=[jax.ShapeDtypeStruct(*out) for out in outs],
        scratch_shapes=[pltpu.VMEM(arg.shape, arg.dtype) for arg in args]
        + [pltpu.VMEM(*out) for out in outs]
        + [pltpu.SemaphoreType.DMA((n_in + n_out,))]
        + [pltpu.VMEM(*item) for item in scratch],
        compiler_params=pltpu.CompilerParams(vmem_limit_bytes=56 * 2**20),
        cost_estimate=pl.CostEstimate(
            flops=cost, bytes_accessed=8 * 2**20, transcendentals=2**19
        ),
    )(*([scalars] * n_at), *args)


ROW, COL, SAME_CORE = ("z", "k"), ("y", "x"), ("z", "y", "x")
SWAP = [(0, 1), (1, 0)]


def turn(value, axis, by):
    size = lax.axis_size(axis)
    return lax.ppermute(value, axis, [(i, i ^ by) for i in range(size)])


def take(value, start, size, axis=0):
    return lax.dynamic_slice_in_dim(value, start, size, axis)


def on_device(
    atom_single, atom_token, atom_cot, token_cond, pair, w_pool, w_qkv, w_bias, w_out, w_dec
):
    side = lax.axis_size("x")
    rows, cols = lax.axis_size("z") * 2, lax.axis_size("y") * side
    z, core, y, x = [lax.axis_index(name) for name in ("z", "k", "y", "x")]
    row, col = z * 2 + core, y * side + x
    tok_rows = token_cond.shape[0]
    total_tokens = tok_rows * rows
    n_atoms, width = atom_single.shape
    tile, columns = tok_rows // cols, total_tokens // cols
    peers = rows * cols // 2
    at = jnp.stack([row, col, z, core]).astype(jnp.int32)
    w_t = jnp.transpose(w_qkv, (0, 2, 1)).reshape(3 * HD, -1)

    ids = jnp.concatenate([atom_token, lax.ppermute(atom_token, "k", SWAP)])
    other_single = lax.ppermute(atom_single, "k", SWAP)
    other_cot = lax.ppermute(atom_cot, "k", SWAP)
    slots = jnp.arange(total_tokens // 2, dtype=jnp.int32)
    slots = (slots // tok_rows * 2 + core) * tok_rows + slots % tok_rows
    partial = 0.0
    for held, single, cot in (
        (ids[:n_atoms], atom_single, atom_cot),
        (ids[n_atoms:], other_single, other_cot),
    ):
        onehot = (slots[:, None] == held[None, :]).astype(BF)
        with_ones = jnp.concatenate([single, cot, jnp.ones_like(single)], axis=1)
        partial = partial + nn(onehot, with_ones)
    partial = partial.reshape(peers, tile, 3 * width)
    place = jnp.eye(tile, width, dtype=F32)
    partial_counts = jnp.sum(partial[:, :, 2 * width :] * place, axis=1, keepdims=True)
    to_tiles = jnp.concatenate(
        [
            partial[:, :, :width].astype(BF),
            partial[:, :, width : 2 * width].astype(BF),
            jnp.pad(partial_counts.astype(BF), ((0, 0), (0, 7), (0, 0))),
        ],
        axis=1,
    )

    first, late_w = tok_rows // 4, after(w_bias, to_tiles)
    biases = [
        jnp.einsum("ijc,ch->hij", part, late_w, preferred_element_type=F32).astype(BF)
        for part in (pair[:first], pair[first:])
    ]
    from_all = exchange(to_tiles, SAME_CORE)
    from_all = after(from_all, *biases)
    sums = jnp.sum(from_all.astype(F32), axis=0)
    tile_counts = jnp.sum(sums[2 * tile : 2 * tile + 1] * place, axis=1, keepdims=True)
    pooled_tile = (sums[:tile] / tile_counts).astype(BF)
    lanes = jnp.arange(width, dtype=jnp.int32)[None]
    seat = jnp.arange(tile, dtype=jnp.int32)[:, None] + tile * (col % (cols // 2))
    count_row = jnp.sum(jnp.where(lanes == seat, tile_counts, 0.0), axis=0, keepdims=True)
    count_row = jnp.where(jnp.arange(8)[:, None] == col // (cols // 2), count_row, 0.0)
    count_row = jnp.pad(count_row[:2], ((0, tile - 2), (0, 0)))
    shared = jnp.concatenate([sums[tile : 2 * tile], count_row], axis=0).astype(BF)
    shared = jnp.broadcast_to(shared[None], (cols, 2 * tile, width))
    pooled = spread(pooled_tile, SAME_CORE)
    late_cond = after(token_cond, biases[0])
    pieces = [turn(late_cond, "z", d) for d in (1, 2, 3)]
    pooled = pooled.reshape(rows // 2, tok_rows, width)
    to_col = after(jnp.concatenate(biases + [shared], axis=1), pooled, *pieces)
    bias_cot = exchange(to_col, COL)
    conds = []
    for piece in [token_cond] + pieces:
        piece = after(piece, to_col)
        conds += [piece, lax.ppermute(piece, "k", SWAP)]
    other_pooled = lax.ppermute(pooled, "k", SWAP)
    single_tile = take(token_cond, col * tile, tile).astype(F32) + nn(pooled_tile, w_pool)
    tile_base = nn(single_tile.astype(BF), w_dec)
    features = w_t.shape[1]
    normed, inverse, kv, queries, queries_t = call(
        norm_kernel,
        [
            ((cols, columns, features), BF),
            ((cols, columns, 1), F32),
            ((cols, 2 * HD, columns), BF),
            ((tok_rows, HD), BF),
            ((HD, tok_rows), BF),
        ],
        [], 10**9, *conds, pooled, other_pooled, w_t, w_pool, scalars=at,
    )
    bias_cot = after(bias_cot, kv, tile_base)
    row_counts = jnp.sum(bias_cot[:, tok_rows + tile : tok_rows + tile + 2].astype(F32), axis=0)
    block_counts = jnp.where(row == col // 2, take(row_counts, col % 2, 1), 0.0).astype(BF)

    spread_logits = (rows, tok_rows, 2 * columns)
    grad_logits, grad_kv, grad_queries, attended, grad_out = call(
        attend_kernel,
        [
            ((cols, tok_rows, columns), BF),
            ((2 * HD, total_tokens), BF),
            ((tok_rows, HD), BF),
            ((tok_rows, HD), BF),
            ((tok_rows, features), F32),
        ],
        [(spread_logits, F32), (spread_logits, F32)],
        2 * 10**9, queries, queries_t, kv, bias_cot, w_out, w_dec,
    )
    bias_back = exchange(grad_logits, COL)
    mine, other, back = call(
        token_grad_kernel,
        [
            ((cols, columns // 2, width), F32),
            ((cols, columns // 2, width), BF),
            ((cols, tile, width), BF),
        ],
        [((cols, columns, features), F32)],
        10**9,
        grad_kv, grad_queries, attended, grad_out, normed, inverse, w_t, w_pool, w_out, w_dec,
        scalars=at,
    )
    grad_part = (mine + lax.ppermute(other, "k", SWAP).astype(F32)).astype(BF)
    to_col = jnp.concatenate([grad_part, back], axis=1)
    bias_back = after(bias_back, to_col)
    hop = exchange(after(to_col, bias_back), COL)
    weight_part = jnp.einsum("ijc,hij->hc", pair, bias_back, preferred_element_type=F32)
    hop = after(hop, weight_part)
    block_counts = block_counts + lax.ppermute(block_counts, "k", SWAP)
    rest = jnp.sum(hop.astype(F32), axis=0)
    heads = weight_part.shape[0]
    to_z = jnp.concatenate(
        [rest[: columns // 2].astype(BF), (tile_base + rest[columns // 2 :]).astype(BF)]
        + high_low(weight_part)
        + [jnp.pad(block_counts, ((0, 15), (0, 0)))],
        axis=0,
    )
    hop = jnp.stack([to_z] + [turn(to_z, "z", d) for d in (1, 2, 3)])
    at_back = columns // 2
    at_weight = at_back + tile
    at_counts = at_weight + 2 * heads
    count_row = jnp.sum(hop[:, at_counts : at_counts + 1].astype(F32), axis=0)
    seats = core * at_back + jnp.arange(at_back, dtype=jnp.int32)[:, None]
    own_counts = jnp.sum(jnp.where(lanes == seats, count_row, 0.0), axis=1, keepdims=True)
    token_grad = (jnp.sum(hop[:, :at_back].astype(F32), axis=0) / own_counts).astype(BF)
    token_back = hop[:, at_back:at_weight].reshape(at_back, width)
    weight_col = jnp.sum(hop[:, at_weight:at_counts].astype(F32), axis=0)
    hop = spread(
        jnp.concatenate(
            [token_grad, token_back] + high_low(weight_col[:heads] + weight_col[heads:]), axis=0
        ),
        COL,
    )
    weight = jnp.sum(hop[:, columns:].astype(F32), axis=0)
    weight = weight[:heads] + weight[heads:]
    grad_table = hop[:, :at_back].reshape(cols * at_back, width)
    back_table = hop[:, at_back:columns].reshape(cols * at_back, width)
    slots = jnp.arange(cols * at_back, dtype=jnp.int32)[None, :]
    of_row, rest = ids // tok_rows, ids % tok_rows
    grad_ids = ids // columns * at_back + ids % at_back
    grad_ids = jnp.where(ids % columns // at_back == core, grad_ids, -1)
    back_ids = rest // tile * at_back + jnp.bitwise_xor(of_row // 2, z) * tile + rest % tile
    back_ids = jnp.where(of_row % 2 == core, back_ids, -1)
    backs = nn((back_ids[:, None] == slots).astype(BF), back_table).astype(BF)
    grads = nn((grad_ids[:, None] == slots).astype(BF), grad_table).astype(BF)
    other_backs = lax.ppermute(backs[n_atoms:], "k", SWAP)
    other_grads = lax.ppermute(grads[n_atoms:], "k", SWAP)
    backs = backs[:n_atoms].astype(F32) + other_backs.astype(F32)
    grads = grads[:n_atoms].astype(F32) + other_grads.astype(F32)
    atom_out = (atom_single.astype(F32) + backs).astype(BF)
    grad_atom = atom_cot.astype(F32) + grads
    grad_bias = jnp.transpose(weight + lax.ppermute(weight, "k", SWAP))
    return (atom_out, grad_atom, grad_bias)


def solution(mesh):
    rows, cols = mesh.devices.shape
    side = math.isqrt(cols)
    devices = mesh.devices.reshape(rows // 2, 2, side, side)
    everyone = ROW + COL
    return jax.shard_map(
        on_device,
        mesh=Mesh(devices, everyone),
        in_specs=(
            P(everyone, None),
            P(everyone),
            P(everyone, None),
            P(ROW, None),
            P(ROW, COL, None),
            P(),
            P(None, None, COL),
            P(),
            P(COL, None),
            P(),
        ),
        out_specs=(P(everyone, None), P(everyone, None), P()),
        check_vma=False,
    )
```

```python
import math

import jax
import jax.numpy as jnp
from jax import lax
from jax.experimental import pallas as pl
from jax.experimental.pallas import tpu as pltpu
from jax.sharding import Mesh
from jax.sharding import PartitionSpec as P

HD = 48


EPSILON = 1e-05
BF = jnp.bfloat16
F32 = jnp.float32


def nt(left, right):
    return lax.dot_general(left, right, (((1,), (1,)), ((), ())), preferred_element_type=F32)


def tn(left, right):
    return lax.dot_general(left, right, (((0,), (0,)), ((), ())), preferred_element_type=F32)


def nn(left, right):
    return jnp.dot(left, right, preferred_element_type=F32)


def exchange(blocks, axis):
    return lax.all_to_all(blocks, axis, split_axis=0, concat_axis=0, tiled=True)


def spread(block, axis):
    return exchange(jnp.broadcast_to(block[None], (lax.axis_size(axis),) + block.shape), axis)


def after(value, *others):
    return lax.optimization_barrier((value,) + others)[0]


def high_low(value):
    high = value.astype(BF)
    return [high, (value - high.astype(F32)).astype(BF)]


def norm_kernel(
    at, cond0, cond1, cond2, cond3, cond4, cond5, cond6, cond7, pooled_ref, pooled_other, wt_ref,
    wpool_ref, normed_ref, inv_ref, kv_ref, q_ref, qt_ref,
):
    cols, half, _ = normed_ref.shape
    conds = (cond0, cond1, cond2, cond3, cond4, cond5, cond6, cond7)
    for step in range(cols // 2):
        at_z = jnp.bitwise_xor(at[2], step // 2)
        b = 2 * at_z + jnp.bitwise_xor(at[3], step % 2)
        pools = pooled_other if step % 2 else pooled_ref
        single = conds[step][...].astype(F32) + nn(pools[at_z], wpool_ref[...])
        center = single - jnp.mean(single, axis=-1, keepdims=True)
        inverse = lax.rsqrt(jnp.mean(center * center, axis=-1, keepdims=True) + EPSILON)
        normed = (center * inverse).astype(BF)
        kv = nt(wt_ref[HD:], normed).astype(BF)
        for i in range(2):
            part = slice(i * half, (i + 1) * half)
            normed_ref[2 * b + i] = normed[part]
            inv_ref[2 * b + i] = inverse[part]
            kv_ref[2 * b + i] = kv[:, part]
        if step == 0:
            q_ref[...] = nt(normed, wt_ref[:HD]).astype(BF)
            qt_ref[...] = nt(wt_ref[:HD], normed).astype(BF)


def attend_kernel(
    q_ref, qt_ref, kv_ref, bias_ref, wout_ref, wdec_ref,
    out_ref, gkv_ref, gq_ref, att_ref, gout_ref, s_ref, g_ref,
):
    scale = 1.0 / math.sqrt(HD)
    blocks, tokens, columns = s_ref.shape
    half = columns // 2
    cols = 2 * blocks
    tile = tokens // cols

    def pair(ref, b, rows):
        return jnp.concatenate([ref[2 * b, rows], ref[2 * b + 1, rows]], axis=1)

    keys, values = slice(0, HD), slice(HD, 2 * HD)
    queries = q_ref[...]
    top = jnp.full((tokens, 1), -jnp.inf, F32)
    for b in range(blocks):
        bias = pair(bias_ref, b, slice(0, tokens))
        logits = nn(queries, pair(kv_ref, b, keys)) * scale + bias.astype(F32)
        s_ref[b] = logits
        top = jnp.maximum(top, jnp.max(logits, axis=-1, keepdims=True))
    total = jnp.zeros((tokens, 1), F32)
    for b in range(blocks):
        shifted = jnp.exp(s_ref[b] - top)
        s_ref[b] = shifted
        total = total + jnp.sum(shifted, axis=-1, keepdims=True)
    share = 1.0 / total

    cots = jnp.concatenate([bias_ref[c, tokens : tokens + tile] for c in range(cols)], axis=0)
    grad_out = nt(cots, wdec_ref[...])
    gout_ref[...] = grad_out
    grad_low = grad_out.astype(BF)
    grad_att = nt(grad_low, wout_ref[...]).astype(BF)
    grad_att_t = nt(wout_ref[...], grad_low).astype(BF)
    attended = jnp.zeros((tokens, HD), F32)
    delta = jnp.zeros((tokens, 1), F32)
    for b in range(blocks):
        probs = s_ref[b] * share
        s_ref[b] = probs
        block = pair(kv_ref, b, values)
        attended = attended + nt(probs.astype(BF), block)
        grad_probs = nn(grad_att, block)
        g_ref[b] = grad_probs
        delta = delta + jnp.sum(probs * grad_probs, axis=-1, keepdims=True)
    att_ref[...] = attended.astype(BF)

    grad_queries = jnp.zeros((tokens, HD), F32)
    for b in range(blocks):
        probs = s_ref[b]
        low = (probs * (g_ref[b] - delta)).astype(BF)
        out_ref[2 * b] = low[:, :half]
        out_ref[2 * b + 1] = low[:, half:]
        grad_queries = grad_queries + nt(low, pair(kv_ref, b, keys))
        grad_k = (nn(qt_ref[...], low) * scale).astype(BF)
        grad_v = nn(grad_att_t, probs.astype(BF)).astype(BF)
        gkv_ref[:, b * columns : (b + 1) * columns] = jnp.concatenate([grad_k, grad_v], axis=0)
    gq_ref[...] = (grad_queries * scale).astype(BF)


def token_grad_kernel(
    at, gkv_ref, gq_ref, att_ref, gout_ref, normed_ref, inv_ref, wt_ref, wpool_ref, wout_ref,
    wdec_ref, mine_ref, other_ref, back_ref, u_ref,
):
    cols, half, _ = normed_ref.shape
    tile, short = back_ref.shape[1], half // 2
    row, col, core = at[0], at[1], at[3]
    update = nn(att_ref[...], wout_ref[...]).astype(BF)
    back = nn(update, wdec_ref[...]).astype(BF)
    for c in range(cols):
        back_ref[c] = back[c * tile : (c + 1) * tile]
    for b in range(cols // 2):
        columns = slice(2 * b * half, 2 * (b + 1) * half)
        upstream = tn(gkv_ref[:, columns], wt_ref[HD:])
        u_ref[2 * b] = upstream[:half]
        u_ref[2 * b + 1] = upstream[half:]
    own = nn(gq_ref[...], wt_ref[:HD])
    u_ref[2 * row] += own[:half]
    u_ref[2 * row + 1] += own[half:]
    head = (col == 0).astype(F32)
    for c in range(cols):
        upstream = u_ref[c]
        normal = normed_ref[c].astype(F32)
        part = inv_ref[c] * (
            upstream
            - jnp.mean(upstream, axis=-1, keepdims=True)
            - normal * jnp.mean(upstream * normal, axis=-1, keepdims=True)
        )
        here = head * (row == c // 2).astype(F32)
        at_half = (c % 2) * half
        part = part + gout_ref[at_half : at_half + half] * here
        grad = nt(part.astype(BF), wpool_ref[...])
        mine_ref[c] = jnp.where(core == 0, grad[:short], grad[short:])
        other_ref[c] = jnp.where(core == 0, grad[short:], grad[:short]).astype(BF)


def call(body, outs, scratch, cost, *args, scalars=None):
    n_in, n_out, n_at = len(args), len(outs), int(scalars is not None)

    def kernel(*refs):
        at, refs = refs[:n_at], refs[n_at:]
        sources, results = refs[:n_in], refs[n_in : n_in + n_out]
        held = refs[n_in + n_out : 2 * (n_in + n_out)]
        sems, rest = refs[2 * (n_in + n_out)], refs[2 * (n_in + n_out) + 1 :]
        incoming = [
            pltpu.make_async_copy(src, dst, sems.at[i])
            for i, (src, dst) in enumerate(zip(sources, held[:n_in]))
        ]
        for copy in incoming:
            copy.start()
        for copy in incoming:
            copy.wait()
        body(*at, *held, *rest)
        outgoing = [
            pltpu.make_async_copy(src, dst, sems.at[n_in + i])
            for i, (src, dst) in enumerate(zip(held[n_in:], results))
        ]
        for copy in outgoing:
            copy.start()
        for copy in outgoing:
            copy.wait()

    anywhere = pl.BlockSpec(memory_space=pl.ANY)
    specs = [pl.BlockSpec(memory_space=pltpu.SMEM)] * n_at + [anywhere] * n_in
    return pl.pallas_call(
        kernel,
        in_specs=specs,
        out_specs=[anywhere] * n_out,
        out_shape=[jax.ShapeDtypeStruct(*out) for out in outs],
        scratch_shapes=[pltpu.VMEM(arg.shape, arg.dtype) for arg in args]
        + [pltpu.VMEM(*out) for out in outs]
        + [pltpu.SemaphoreType.DMA((n_in + n_out,))]
        + [pltpu.VMEM(*item) for item in scratch],
        compiler_params=pltpu.CompilerParams(vmem_limit_bytes=56 * 2**20),
        cost_estimate=pl.CostEstimate(
            flops=cost, bytes_accessed=8 * 2**20, transcendentals=2**19
        ),
    )(*([scalars] * n_at), *args)


ROW, COL, SAME_CORE = ("z", "k"), ("y", "x"), ("z", "y", "x")
SWAP = [(0, 1), (1, 0)]


def turn(value, axis, by):
    size = lax.axis_size(axis)
    return lax.ppermute(value, axis, [(i, i ^ by) for i in range(size)])


def take(value, start, size, axis=0):
    return lax.dynamic_slice_in_dim(value, start, size, axis)


def on_device(
    atom_single, atom_token, atom_cot, token_cond, pair, w_pool, w_qkv, w_bias, w_out, w_dec
):
    side = lax.axis_size("x")
    rows, cols = lax.axis_size("z") * 2, lax.axis_size("y") * side
    z, core, y, x = [lax.axis_index(name) for name in ("z", "k", "y", "x")]
    row, col = z * 2 + core, y * side + x
    tok_rows = token_cond.shape[0]
    total_tokens = tok_rows * rows
    n_atoms, width = atom_single.shape
    tile, columns = tok_rows // cols, total_tokens // cols
    peers = rows * cols // 2
    at = jnp.stack([row, col, z, core]).astype(jnp.int32)
    w_t = jnp.transpose(w_qkv, (0, 2, 1)).reshape(3 * HD, -1)

    ids = jnp.concatenate([atom_token, lax.ppermute(atom_token, "k", SWAP)])
    other_single = lax.ppermute(atom_single, "k", SWAP)
    other_cot = lax.ppermute(atom_cot, "k", SWAP)
    slots = jnp.arange(total_tokens // 2, dtype=jnp.int32)
    slots = (slots // tok_rows * 2 + core) * tok_rows + slots % tok_rows
    partial = 0.0
    for held, single, cot in (
        (ids[:n_atoms], atom_single, atom_cot),
        (ids[n_atoms:], other_single, other_cot),
    ):
        onehot = (slots[:, None] == held[None, :]).astype(BF)
        with_ones = jnp.concatenate([single, cot, jnp.ones_like(single)], axis=1)
        partial = partial + nn(onehot, with_ones)
    partial = partial.reshape(peers, tile, 3 * width)
    place = jnp.eye(tile, width, dtype=F32)
    partial_counts = jnp.sum(partial[:, :, 2 * width :] * place, axis=1, keepdims=True)
    to_tiles = jnp.concatenate(
        [
            partial[:, :, :width].astype(BF),
            partial[:, :, width : 2 * width].astype(BF),
            jnp.pad(partial_counts.astype(BF), ((0, 0), (0, 7), (0, 0))),
        ],
        axis=1,
    )

    first, late_w = tok_rows // 4, after(w_bias, to_tiles)
    biases = [
        jnp.einsum("ijc,ch->hij", part, late_w, preferred_element_type=F32).astype(BF)
        for part in (pair[:first], pair[first:])
    ]
    from_all = exchange(to_tiles, SAME_CORE)
    from_all = after(from_all, *biases)
    sums = jnp.sum(from_all.astype(F32), axis=0)
    tile_counts = jnp.sum(sums[2 * tile : 2 * tile + 1] * place, axis=1, keepdims=True)
    pooled_tile = (sums[:tile] / tile_counts).astype(BF)
    lanes = jnp.arange(width, dtype=jnp.int32)[None]
    seat = jnp.arange(tile, dtype=jnp.int32)[:, None] + tile * (col % (cols // 2))
    count_row = jnp.sum(jnp.where(lanes == seat, tile_counts, 0.0), axis=0, keepdims=True)
    count_row = jnp.where(jnp.arange(8)[:, None] == col // (cols // 2), count_row, 0.0)
    count_row = jnp.pad(count_row[:2], ((0, tile - 2), (0, 0)))
    shared = jnp.concatenate([sums[tile : 2 * tile], count_row], axis=0).astype(BF)
    shared = jnp.broadcast_to(shared[None], (cols, 2 * tile, width))
    pooled = spread(pooled_tile, SAME_CORE)
    late_cond = after(token_cond, biases[0])
    pieces = [turn(late_cond, "z", d) for d in (1, 2, 3)]
    pooled = pooled.reshape(rows // 2, tok_rows, width)
    to_col = after(jnp.concatenate(biases + [shared], axis=1), pooled, *pieces)
    bias_cot = exchange(to_col, COL)
    conds = []
    for piece in [token_cond] + pieces:
        piece = after(piece, to_col)
        conds += [piece, lax.ppermute(piece, "k", SWAP)]
    other_pooled = lax.ppermute(pooled, "k", SWAP)
    single_tile = take(token_cond, col * tile, tile).astype(F32) + nn(pooled_tile, w_pool)
    tile_base = nn(single_tile.astype(BF), w_dec)
    features = w_t.shape[1]
    normed, inverse, kv, queries, queries_t = call(
        norm_kernel,
        [
            ((cols, columns, features), BF),
            ((cols, columns, 1), F32),
            ((cols, 2 * HD, columns), BF),
            ((tok_rows, HD), BF),
            ((HD, tok_rows), BF),
        ],
        [], 10**9, *conds, pooled, other_pooled, w_t, w_pool, scalars=at,
    )
    bias_cot = after(bias_cot, kv, tile_base)
    row_counts = jnp.sum(bias_cot[:, tok_rows + tile : tok_rows + tile + 2].astype(F32), axis=0)
    block_counts = jnp.where(row == col // 2, take(row_counts, col % 2, 1), 0.0).astype(BF)

    spread_logits = (rows, tok_rows, 2 * columns)
    grad_logits, grad_kv, grad_queries, attended, grad_out = call(
        attend_kernel,
        [
            ((cols, tok_rows, columns), BF),
            ((2 * HD, total_tokens), BF),
            ((tok_rows, HD), BF),
            ((tok_rows, HD), BF),
            ((tok_rows, features), F32),
        ],
        [(spread_logits, F32), (spread_logits, F32)],
        2 * 10**9, queries, queries_t, kv, bias_cot, w_out, w_dec,
    )
    bias_back = exchange(grad_logits, COL)
    mine, other, back = call(
        token_grad_kernel,
        [
            ((cols, columns // 2, width), F32),
            ((cols, columns // 2, width), BF),
            ((cols, tile, width), BF),
        ],
        [((cols, columns, features), F32)],
        10**9,
        grad_kv, grad_queries, attended, grad_out, normed, inverse, w_t, w_pool, w_out, w_dec,
        scalars=at,
    )
    grad_part = (mine + lax.ppermute(other, "k", SWAP).astype(F32)).astype(BF)
    to_col = jnp.concatenate([grad_part, back], axis=1)
    bias_back = after(bias_back, to_col)
    hop = exchange(after(to_col, bias_back), COL)
    weight_part = jnp.einsum("ijc,hij->hc", pair, bias_back, preferred_element_type=F32)
    hop = after(hop, weight_part)
    block_counts = block_counts + lax.ppermute(block_counts, "k", SWAP)
    rest = jnp.sum(hop.astype(F32), axis=0)
    heads = weight_part.shape[0]
    to_z = jnp.concatenate(
        [rest[: columns // 2].astype(BF), (tile_base + rest[columns // 2 :]).astype(BF)]
        + high_low(weight_part)
        + [jnp.pad(block_counts, ((0, 7), (0, 0)))],
        axis=0,
    )
    hop = jnp.stack([to_z] + [turn(to_z, "z", d) for d in (1, 2, 3)])
    at_back = columns // 2
    at_weight = at_back + tile
    at_counts = at_weight + 2 * heads
    count_row = jnp.sum(hop[:, at_counts : at_counts + 1].astype(F32), axis=0)
    seats = core * at_back + jnp.arange(at_back, dtype=jnp.int32)[:, None]
    own_counts = jnp.sum(jnp.where(lanes == seats, count_row, 0.0), axis=1, keepdims=True)
    token_grad = (jnp.sum(hop[:, :at_back].astype(F32), axis=0) / own_counts).astype(BF)
    token_back = hop[:, at_back:at_weight].reshape(at_back, width)
    weight_col = jnp.sum(hop[:, at_weight:at_counts].astype(F32), axis=0)
    hop = spread(
        jnp.concatenate(
            [token_grad, token_back] + high_low(weight_col[:heads] + weight_col[heads:]), axis=0
        ),
        COL,
    )
    weight = jnp.sum(hop[:, columns:].astype(F32), axis=0)
    weight = weight[:heads] + weight[heads:]
    grad_table = hop[:, :at_back].reshape(cols * at_back, width)
    back_table = hop[:, at_back:columns].reshape(cols * at_back, width)
    slots = jnp.arange(cols * at_back, dtype=jnp.int32)[None, :]
    of_row, rest = ids // tok_rows, ids % tok_rows
    grad_ids = ids // columns * at_back + ids % at_back
    grad_ids = jnp.where(ids % columns // at_back == core, grad_ids, -1)
    back_ids = rest // tile * at_back + jnp.bitwise_xor(of_row // 2, z) * tile + rest % tile
    back_ids = jnp.where(of_row % 2 == core, back_ids, -1)
    backs = nn((back_ids[:, None] == slots).astype(BF), back_table).astype(BF)
    grads = nn((grad_ids[:, None] == slots).astype(BF), grad_table).astype(BF)
    other_backs = lax.ppermute(backs[n_atoms:], "k", SWAP)
    other_grads = lax.ppermute(grads[n_atoms:], "k", SWAP)
    backs = backs[:n_atoms].astype(F32) + other_backs.astype(F32)
    grads = grads[:n_atoms].astype(F32) + other_grads.astype(F32)
    atom_out = (atom_single.astype(F32) + backs).astype(BF)
    grad_atom = atom_cot.astype(F32) + grads
    grad_bias = jnp.transpose(weight + lax.ppermute(weight, "k", SWAP))
    return (atom_out, grad_atom, grad_bias)


def solution(mesh):
    rows, cols = mesh.devices.shape
    side = math.isqrt(cols)
    devices = mesh.devices.reshape(rows // 2, 2, side, side)
    everyone = ROW + COL
    return jax.shard_map(
        on_device,
        mesh=Mesh(devices, everyone),
        in_specs=(
            P(everyone, None),
            P(everyone),
            P(everyone, None),
            P(ROW, None),
            P(ROW, COL, None),
            P(),
            P(None, None, COL),
            P(),
            P(COL, None),
            P(),
        ),
        out_specs=(P(everyone, None), P(everyone, None), P()),
        check_vma=False,
    )
```
